32 devices in a mesh: sec: 2 (over y), dev: 16 (over z, x, core).
Axes of the slice: x: 2, y: 2, z: 4, core: 2. Of those that a mesh axis runs over, the one named last changes fastest.
Arguments:
- hidden_in: bfloat16 [512, 7168], P(('sec', 'dev')), may hold values from -6 to 6
- expert_ids: int32 [512, 8], P(('sec', 'dev')), may hold values from 0 to 15, all different within a row; in each aligned block of 8 rows (0 to 7, 8 to 15, ...) at most 8 rows name the same one
- gate_coef: float32 [512, 8], P(('sec', 'dev')), may hold values from 0.1 to 1
- query_lat: bfloat16 [512, 64, 576], P(('sec', 'dev')), may hold values from -40 to 40
- kv_cache: bfloat16 [512, 128, 576], P(('sec', 'dev')), may hold values from -6 to 6
- cache_len: int32 [512], P(('sec', 'dev')), may hold values from 32 to 128, as said below
- gate_weight: bfloat16 [16, 7168, 1024], P('dev', None, 'sec'), may hold values from -0.0625 to 0.0625
- up_weight: bfloat16 [16, 7168, 1024], P('dev', None, 'sec'), may hold values from -0.0625 to 0.0625
- down_weight: bfloat16 [16, 1024, 7168], P('dev', 'sec'), may hold values from -0.1875 to 0.1875
Outputs:
- attention: bfloat16 [512, 64, 512], P(('sec', 'dev'))
- routed_out: bfloat16 [512, 7168], P(('sec', 'dev'))
The draws below stay inside these ranges and needn't reach their ends.
Inputs may be any that keep to these rules, and one draw needn't show every extreme that they name: `expert_ids`: each row names 8 different experts. In each aligned block of 8 rows (one micro-batch of one device) no expert is named by more than 8 rows, and in some block an expert is named by exactly 8 rows. `cache_len`: some row uses all 128 slots.
All inputs are finite; a program needn't handle non-finite values.
Results may differ from the reference program's by a relative error of at most 0.0065.
Values may be sent and summed in bfloat16 or wider, within the bound.
No kernel may reach another device: no remote copies, remote signals or barrier semaphores. Data moves between devices by JAX's collectives and lax.ppermute only.
A program may use at most 128 MiB of HBM per device.

```python
import math
import jax
import jax.numpy as jnp
import numpy as np
from jax import lax

D = 7168
FF = 1024
HEADS = 64
LAT = 512
ROPE = 64
TOP = 8
CTX = 128
MB_ROWS = 8
ROWS = 512
EXPERTS = 16
CAP = 8
N_SEC = 2


def latent_pair(key):
    base = jax.random.fold_in(key, 7)
    keys = jax.random.split(base, 2)
    width = LAT + ROPE
    cache_vals = jnp.clip(jax.random.normal(keys[0], (ROWS, CTX, width), jnp.float32), -5.0, 5.0)
    query_vals = jnp.clip(jax.random.normal(keys[1], (ROWS, HEADS, width), jnp.float32), -5.0, 5.0)
    return (cache_vals, query_vals)


def draw_query_lat(key, part):
    cache_vals, query_vals = latent_pair(key)
    return query_vals.astype(jnp.bfloat16)


def draw_kv_cache(key, part):
    cache_vals, query_vals = latent_pair(key)
    return cache_vals.astype(jnp.bfloat16)


def draw_cache_len(key, part):
    keys = jax.random.split(jax.random.fold_in(key, 11), 2)
    lengths = jax.random.randint(keys[0], (ROWS,), CTX // 4, CTX + 1)
    full_row = jax.random.randint(keys[1], (), 0, ROWS)
    return jnp.where(jnp.arange(ROWS) == full_row, CTX, lengths).astype(jnp.int32)


def steps_of(rng, extent, cuts, least, top_value):
    def one(position, shards_of):
        heights = jax.random.uniform(jax.random.fold_in(jax.random.fold_in(rng, 6), position), (shards_of,), jnp.float32, least / len(cuts), top_value / len(cuts))
        return jnp.repeat(jnp.exp(heights), extent[position] // shards_of).reshape((-1,) + (1,) * (len(extent) - position - 1))

    factor_of = one(*cuts[0])
    for cut in cuts[1:]:
        factor_of = factor_of * one(*cut)
    return factor_of


def routed_block(key, own, number, rows, amount, top, most, slope):
    sequence = jax.random.permutation(key, amount)
    crowded, ordinary = shares(amount, rows * top, most, slope, True), shares(amount, rows * top, most, slope, False)
    places = jnp.arange(amount)

    def named(sizes, turn):
        used = int((sizes > 0).sum())
        fixed = max(1, used // 4)
        shifted = fixed + (places - fixed + turn * (used - fixed)) % max(1, amount - fixed)
        return jnp.zeros((amount,), jnp.int32).at[sequence[jnp.where(places < fixed, places, shifted)]].set(jnp.asarray(sizes, jnp.int32))

    sizes = jnp.where(number % 4 == 0, named(crowded, number // 4), named(ordinary, number - number // 4 - 1))
    mixed = jax.random.permutation(jax.random.fold_in(own, 3), amount)
    donor, sink = mixed[0:amount // 2 * 2:2], mixed[1:amount // 2 * 2:2]
    margin = jnp.minimum(sizes[donor] - 1, most - sizes[sink]) // 2
    margin = jnp.where((donor == sequence[0]) | (sink == sequence[0]) | (sizes[sink] == 0), 0, jnp.maximum(margin, 0))
    shifted = jax.random.randint(jax.random.fold_in(own, 4), (amount // 2,), 0, 1 << 20) % (margin + 1)
    sizes = sizes.at[donor].add(-shifted).at[sink].add(shifted)
    labels = jnp.searchsorted(jnp.cumsum(sizes), jnp.arange(rows * top), side="right").astype(jnp.int32)
    listing = labels.reshape(top, rows).T
    listing = listing[jax.random.permutation(jax.random.fold_in(own, 1), rows)]
    turn = jax.random.randint(jax.random.fold_in(own, 2), (rows, 1), 0, top)
    return jnp.take_along_axis(listing, (jnp.arange(top)[None, :] + turn) % top, axis=1)


def shares(number_of, total, most, slope, full):
    weights = [(1 << 20) // math.isqrt(rank ** slope) + 1 for rank in range(1, number_of + 1)]
    largest = most if full else min(most, max(-(-total // number_of), total * weights[0] // sum(weights)))
    least = 1 if total - largest >= number_of - 1 else 0
    holding, rest = [largest] + [least] * (number_of - 1), total - largest - least * (number_of - 1)
    while rest > 0:
        candidates = [i for i in range(1, number_of) if holding[i] < largest] or [i for i in range(1, number_of) if holding[i] < most]
        whole, budget = sum([weights[i] for i in candidates]), rest
        for i in candidates:
            extra = min(most - holding[i], max(1, budget * weights[i] // whole), rest)
            holding[i] = holding[i] + extra
            rest = rest - extra
    return np.array(holding)


def bell_draw(stream_key, dims, scale, bound, shards=(), kind=jnp.bfloat16):
    values = scale * jax.random.normal(stream_key, dims, jnp.float32)
    if shards:
        values = values * steps_of(stream_key, dims, shards, -0.22, 0.18)
    return jnp.clip(values, -bound, bound).astype(kind)


def setup_inputs(seed: int = 0) -> dict:
    seeds = jax.random.split(jax.random.key(seed), 10)
    hidden_in = bell_draw(seeds[0], (ROWS, D), 1.0, 6.0, ((0, 32),))
    expert_ids_keys = jax.random.split(jax.random.fold_in(seeds[1], 1), ROWS // MB_ROWS)
    expert_ids_turns = jax.random.permutation(jax.random.fold_in(seeds[1], 3), ROWS // MB_ROWS)
    expert_ids = jax.vmap(lambda own, number: routed_block(jax.random.fold_in(seeds[1], 2), own, number, MB_ROWS, EXPERTS, TOP, CAP, 2))(expert_ids_keys, expert_ids_turns).reshape((ROWS, TOP))
    gate_coef = jnp.clip(0.1 + 0.9 * jax.random.uniform(seeds[2], (ROWS, TOP), jnp.float32) ** steps_of(seeds[2], (ROWS, TOP), ((0, 32),), -0.2, 0.2), 0.1, 1.0)
    query_lat = draw_query_lat(jax.random.fold_in(seeds[9], 71), 0)
    kv_cache = draw_kv_cache(jax.random.fold_in(seeds[9], 71), 0)
    cache_len = draw_cache_len(jax.random.fold_in(seeds[9], 71), 0)
    gate_weight = bell_draw(seeds[6], (EXPERTS, D, FF), D ** -0.5, 0.0625, ((0, 16), (2, 2)))
    up_weight = bell_draw(seeds[7], (EXPERTS, D, FF), D ** -0.5, 0.0625, ((0, 16), (2, 2)))
    down_weight = bell_draw(seeds[8], (EXPERTS, FF, D), FF ** -0.5, 0.1875, ((0, 16), (1, 2)))
    return dict(hidden_in=hidden_in, expert_ids=expert_ids, gate_coef=gate_coef, query_lat=query_lat, kv_cache=kv_cache, cache_len=cache_len, gate_weight=gate_weight, up_weight=up_weight, down_weight=down_weight)


score_scale = 1.0 / math.sqrt(192.0)

def attend(query_lat, kv_cache, cache_len):
    query_f = query_lat.astype(jnp.float32)
    cache_f = kv_cache.astype(jnp.float32)
    scores = jnp.einsum('rhk,rlk->rhl', query_f, cache_f) * score_scale
    positions = jnp.arange(kv_cache.shape[1], dtype=jnp.int32)
    visible = positions[None, None, :] < cache_len[:, None, None]
    scores = jnp.where(visible, scores, jnp.float32(-1e+30))
    top_score = lax.optimization_barrier(jnp.max(scores, axis=2, keepdims=True))
    exponent = jnp.exp(scores - top_score)
    denominator = lax.optimization_barrier(jnp.sum(exponent, axis=2, keepdims=True))
    weights = (exponent / denominator).astype(jnp.bfloat16)
    output = jnp.einsum('rhl,rlc->rhc', weights.astype(jnp.float32), cache_f[:, :, :LAT])
    return output.astype(jnp.bfloat16)

def reference(hidden_in, expert_ids, gate_coef, query_lat, kv_cache, cache_len, gate_weight, up_weight, down_weight):
    attention = attend(query_lat, kv_cache, cache_len)
    block_count = ROWS // MB_ROWS
    per_block = MB_ROWS * TOP
    block_ids = expert_ids.reshape(block_count, per_block).astype(jnp.int32)
    position_ids = jnp.arange(per_block, dtype=jnp.int32)
    matches = (block_ids[:, :, None] == block_ids[:, None, :]) & (position_ids[None, None, :] < position_ids[None, :, None])
    slot_rank = lax.optimization_barrier(jnp.sum(matches.astype(jnp.int32), axis=2)).astype(jnp.int32)
    per_expert = block_count * CAP
    block_base = jnp.arange(block_count, dtype=jnp.int32)[:, None] * CAP
    target = (block_ids * per_expert + block_base + slot_rank).reshape(-1).astype(jnp.int32)
    owner_rows = (jnp.arange(ROWS * TOP, dtype=jnp.int32) // TOP).astype(jnp.int32)
    table = jnp.full((EXPERTS * per_expert,), ROWS, jnp.int32).at[target].set(owner_rows)
    table = table.reshape(EXPERTS, per_expert)
    padded = jnp.concatenate([hidden_in, jnp.zeros((1, D), jnp.bfloat16)], axis=0)
    half_width = FF // N_SEC

    def one_expert(packed):
        row_index, gate_e, up_e, down_e = packed
        tokens = padded[row_index]
        gate_val = jnp.dot(tokens, gate_e, preferred_element_type=jnp.float32)
        up_val = jnp.dot(tokens, up_e, preferred_element_type=jnp.float32)
        hidden = (jax.nn.silu(gate_val) * up_val).astype(jnp.bfloat16)
        running = jnp.zeros((tokens.shape[0], D), jnp.float32)
        for half_index in range(N_SEC):
            lower = half_index * half_width
            part_out = jnp.dot(hidden[:, lower:lower + half_width], down_e[lower:lower + half_width], preferred_element_type=jnp.float32)
            running = running + part_out.astype(jnp.bfloat16).astype(jnp.float32)
        return running.astype(jnp.bfloat16)
    outputs = lax.map(one_expert, (table, gate_weight, up_weight, down_weight))
    flat_out = outputs.reshape(-1, D)
    picked = flat_out[target].astype(jnp.float32).reshape(ROWS, TOP, D)
    routed_out = lax.optimization_barrier(jnp.sum(picked * gate_coef.astype(jnp.float32)[:, :, None], axis=1)).astype(jnp.bfloat16)
    return (attention, routed_out)
```

```python
import math

import jax
import jax.numpy as jnp
from jax import lax
from jax.sharding import PartitionSpec as P

LAT = 512
TOP = 8
AXES = ("sec", "dev")

score_scale = 1.0 / math.sqrt(192.0)


def attend(query_lat, kv_cache, cache_len):
    scores = (
        jnp.einsum("rhk,rlk->rhl", query_lat, kv_cache, preferred_element_type=jnp.float32)
        * score_scale
    )
    positions = jnp.arange(kv_cache.shape[1], dtype=jnp.int32)
    visible = positions[None, None, :] < cache_len[:, None, None]
    scores = jnp.where(visible, scores, jnp.float32(-1e30))
    top_score = jnp.max(scores, axis=2, keepdims=True)
    exponent = jnp.exp(scores - top_score)
    denominator = jnp.sum(exponent, axis=2, keepdims=True)
    weights = (exponent / denominator).astype(jnp.bfloat16)
    return jnp.einsum(
        "rhl,rlc->rhc", weights, kv_cache[:, :, :LAT], preferred_element_type=jnp.float32
    ).astype(jnp.bfloat16)


def routing_tables(expert_ids, gate_coef, expert_count, capacity):
    row_count, top_count = expert_ids.shape
    flat_ids = expert_ids.reshape(-1)
    position_ids = jnp.arange(flat_ids.shape[0], dtype=jnp.int32)
    matches = (flat_ids[:, None] == flat_ids[None, :]) & (
        position_ids[None, :] < position_ids[:, None]
    )
    slot_rank = jnp.sum(matches.astype(jnp.int32), axis=1)
    target = flat_ids * capacity + slot_rank
    slot_ids = jnp.arange(expert_count * capacity, dtype=jnp.int32)
    placed = (target[None, :] == slot_ids[:, None]).astype(jnp.float32)
    owner_hot = (
        (position_ids // top_count)[:, None] == jnp.arange(row_count, dtype=jnp.int32)[None, :]
    ).astype(jnp.float32)
    picker = jnp.dot(placed, owner_hot, precision=lax.Precision.HIGHEST).astype(jnp.bfloat16)
    weighted = owner_hot * gate_coef.reshape(-1)[:, None]
    mixing = jnp.dot(weighted.T, placed.T, precision=lax.Precision.HIGHEST)
    return (picker, mixing)


def expert_rows(tokens, gate_weight, up_weight, down_weight):
    shape_in = tokens.shape
    flat_rows = tokens.reshape(-1, shape_in[-1])
    gate_val = jnp.dot(flat_rows, gate_weight[0], preferred_element_type=jnp.float32)
    up_val = jnp.dot(flat_rows, up_weight[0], preferred_element_type=jnp.float32)
    hidden = (jax.nn.silu(gate_val) * up_val).astype(jnp.bfloat16)
    part_out = jnp.dot(hidden, down_weight[0], preferred_element_type=jnp.float32).astype(
        jnp.bfloat16
    )
    return part_out.reshape(shape_in)


def route_tokens(send_buf, gate_weight, up_weight, down_weight):
    section_count = lax.axis_size("sec")
    doubled = jnp.concatenate([send_buf] * section_count, axis=0)
    halves = expert_rows(
        lax.all_to_all(doubled, AXES, split_axis=0, concat_axis=0, tiled=True),
        gate_weight,
        up_weight,
        down_weight,
    )
    returned = lax.all_to_all(halves, AXES, split_axis=0, concat_axis=0, tiled=True)
    pieces = returned.reshape((section_count,) + send_buf.shape).astype(jnp.float32)
    return jnp.sum(pieces, axis=0).astype(jnp.bfloat16)


def combine(returned, mixing):
    flat_back = returned.reshape(-1, returned.shape[-1]).astype(jnp.float32)
    return jnp.dot(mixing, flat_back, precision=lax.Precision.HIGHEST).astype(jnp.bfloat16)


def routed_sparse(
    hidden_in, expert_ids, gate_coef, gate_weight, up_weight, down_weight, half_rows, capacity
):
    model_width = hidden_in.shape[1]
    expert_count = lax.axis_size("dev")
    outs = []
    for offset in (0, half_rows):
        picker, mixing = routing_tables(
            expert_ids[offset : offset + half_rows],
            gate_coef[offset : offset + half_rows],
            expert_count,
            capacity,
        )
        gathered = jnp.dot(
            picker, hidden_in[offset : offset + half_rows], preferred_element_type=jnp.float32
        ).astype(jnp.bfloat16)
        send_buf = gathered.reshape(expert_count, capacity, model_width)
        outs.append(combine(route_tokens(send_buf, gate_weight, up_weight, down_weight), mixing))
    return jnp.concatenate(outs, axis=0)


def permutation(n_dev, move):
    pairs = []
    for y in range(2):
        for d in range(n_dev):
            there = move(y, d // 4, (d // 2) % 2, d % 2)
            if there is not None:
                ty, tz, tx, tc = there
                pairs.append((y * n_dev + d, ty * n_dev + tz * 4 + tx * 2 + tc))
    return lambda a: lax.ppermute(a, AXES, pairs)


class Moves:
    def __init__(self, n_dev):
        line = n_dev // 4

        def along(y, z, x, c):
            t = z + (1 if c else -1)
            return (y, t, x, c) if 0 <= t < line else None

        self.line = line
        self.core = permutation(n_dev, lambda y, z, x, c: (y, z, x, 1 - c))
        self.first = permutation(
            n_dev, lambda y, z, x, c: (1 - y, z, x, c) if c else (y, z, 1 - x, c)
        )
        self.second = permutation(
            n_dev, lambda y, z, x, c: (y, z, 1 - x, c) if c else (1 - y, z, x, c)
        )
        self.along = permutation(n_dev, along)
        dev = lax.axis_index("dev")
        self.core0 = dev % 2 == 0
        self.place = dev // 4


def swap_halves(a):
    half = a.shape[0] // 2
    return jnp.concatenate([a[half:], a[:half]], axis=0)


def plane_gather(mv, block):
    one = mv.first(block)
    two = mv.second(block)
    both = mv.second(one)
    own = [block, one, two, both]
    return own, [mv.core(b) for b in own]


def pick_slot(mv, k, mine, theirs):
    n = mv.line
    up = jnp.where(mv.core0, mine[k - 1], theirs[k - 1])
    down = jnp.where(mv.core0, theirs[n - k - 1], mine[n - k - 1])
    return jnp.where(mv.place + k < n, up, down)


def gather_line_first(mv, block):
    rows = block.shape[0]
    moving = jnp.concatenate([block, mv.core(block)], axis=0)
    mine, theirs = [], []
    for _ in range(mv.line - 1):
        moving = mv.along(moving)
        mine.append(moving[:rows])
        theirs.append(mv.core(moving[rows:]))
    slots = [block] + [pick_slot(mv, k, mine, theirs) for k in range(1, mv.line)]
    own, other = plane_gather(mv, jnp.concatenate(slots, axis=0))
    return jnp.concatenate(own + other, axis=0)


def gather_plane_first(mv, block):
    own, other = plane_gather(mv, block)
    chip = jnp.concatenate(own + other, axis=0)
    moving = chip
    mine, theirs = [], []
    for _ in range(mv.line - 1):
        moving = mv.along(moving)
        mine.append(moving)
        theirs.append(swap_halves(mv.core(moving)))
    slots = [chip] + [pick_slot(mv, k, mine, theirs) for k in range(1, mv.line)]
    rows, width = block.shape
    stacked = jnp.stack([s.reshape(8, rows, width) for s in slots], axis=1)
    return stacked.reshape(-1, width)


def plus(*terms):
    total = terms[0].astype(jnp.float32)
    for t in terms[1:]:
        total = total + t.astype(jnp.float32)
    return total.astype(jnp.bfloat16)


def plane_sum(mv, s):
    s1 = plus(s[1], mv.second(s[3]))
    return plus(s[0], mv.second(s[2]), mv.first(s1))


def sum_line_last(mv, y):
    n = mv.line
    groups = y.reshape(2, 4, -1, y.shape[1])
    s = [plus(groups[0, i], mv.core(groups[1, i])) for i in range(4)]
    slots = plane_sum(mv, s).reshape(n, -1, y.shape[1])
    rows = slots.shape[1]
    acc = None
    for k in range(n - 1, 0, -1):
        give = jnp.where(mv.core0, slots[k], slots[n - k])
        keep = jnp.where(mv.core0, slots[n - k], slots[k])
        term = jnp.concatenate([keep, mv.core(give)], axis=0)
        acc = mv.along(term if acc is None else plus(term, acc))
    return plus(slots[0], acc[:rows], mv.core(acc[rows:]))


def sum_line_first(mv, y):
    n = mv.line
    width = y.shape[1]
    slots = y.reshape(8, n, -1, width)
    slots = [slots[:, k].reshape(-1, width) for k in range(n)]
    acc = None
    for k in range(n - 1, 0, -1):
        give = jnp.where(mv.core0, slots[k], slots[n - k])
        keep = jnp.where(mv.core0, slots[n - k], slots[k])
        term = (keep, swap_halves(mv.core(give)))
        acc = mv.along(plus(*term) if acc is None else plus(*term, acc))
    half = acc.shape[0] // 2
    t = plus(slots[0], acc)
    s = plus(t[:half], mv.core(t[half:])).reshape(4, -1, width)
    return plane_sum(mv, [s[i] for i in range(4)])


def spread_coefs(expert_ids, gate_coef, expert_count):
    hot = expert_ids[:, :, None] == jnp.arange(expert_count, dtype=jnp.int32)[None, None, :]
    dense = jnp.sum(jnp.where(hot, gate_coef[:, :, None], 0.0), axis=1)
    high = lax.reduce_precision(dense, 8, 7)
    parts = jnp.concatenate([high, dense - high], axis=1).astype(jnp.bfloat16)
    pad = -parts.shape[1] % 128
    return jnp.pad(parts, ((0, 0), (0, pad)))


def routed_dense(hidden_in, expert_ids, gate_coef, gate_weight, up_weight, down_weight):
    width = hidden_in.shape[1]
    n_dev = lax.axis_size("dev")
    mv = Moves(n_dev)
    cut = width // 256 * 9 // 28 * 256
    coefs = spread_coefs(expert_ids, gate_coef, n_dev)
    rows_q = gather_line_first(mv, jnp.concatenate([hidden_in[:, cut:], coefs], axis=1))
    rows_p = gather_plane_first(mv, hidden_in[:, :cut])
    me = lax.axis_index("dev")
    tail = rows_q[:, width - cut :].astype(jnp.float32)
    coef = lax.dynamic_slice_in_dim(tail, me, 1, 1) + lax.dynamic_slice_in_dim(
        tail, me + n_dev, 1, 1
    )
    rows_q = rows_q[:, : width - cut]

    def project(w):
        return jnp.dot(rows_p, w[0, :cut], preferred_element_type=jnp.float32) + jnp.dot(
            rows_q, w[0, cut:], preferred_element_type=jnp.float32
        )

    hidden = (jax.nn.silu(project(gate_weight)) * project(up_weight)).astype(jnp.bfloat16)
    y_q = jnp.dot(hidden, down_weight[0, :, cut:], preferred_element_type=jnp.float32)
    y_p = jnp.dot(hidden, down_weight[0, :, :cut], preferred_element_type=jnp.float32)
    out_q = sum_line_last(mv, (y_q * coef).astype(jnp.bfloat16))
    out_p = sum_line_first(mv, (y_p * coef).astype(jnp.bfloat16))
    return jnp.concatenate([out_p, out_q], axis=1)


def per_device(
    hidden_in,
    expert_ids,
    gate_coef,
    query_lat,
    kv_cache,
    cache_len,
    gate_weight,
    up_weight,
    down_weight,
):
    half_rows = hidden_in.shape[0] // 2
    expert_count = lax.axis_size("dev")
    capacity = max(2, 2 * TOP * half_rows // expert_count)
    weights = (gate_weight, up_weight, down_weight)
    if capacity < half_rows:
        routed_out = routed_sparse(
            hidden_in, expert_ids, gate_coef, *weights, half_rows, capacity
        )
    else:
        routed_out = routed_dense(hidden_in, expert_ids, gate_coef, *weights)
    attention = attend(query_lat, kv_cache, cache_len)
    return (attention, routed_out)


def solution(mesh):
    in_specs = (
        P(("sec", "dev"), None),
        P(("sec", "dev"), None),
        P(("sec", "dev"), None),
        P(("sec", "dev"), None, None),
        P(("sec", "dev"), None, None),
        P(("sec", "dev")),
        P("dev", None, "sec"),
        P("dev", None, "sec"),
        P("dev", "sec", None),
    )
    out_specs = (P(("sec", "dev"), None, None), P(("sec", "dev"), None))
    return jax.shard_map(
        per_device, mesh=mesh, in_specs=in_specs, out_specs=out_specs, check_vma=False
    )
```

```python
import functools
import math

import jax
import jax.numpy as jnp
from jax import lax
from jax.experimental import pallas as pl
from jax.experimental.pallas import tpu as pltpu
from jax.sharding import PartitionSpec as P

LAT = 512
TOP = 8
AXES = ("sec", "dev")

score_scale = 1.0 / math.sqrt(192.0)


def attend(query_lat, kv_cache, cache_len):
    scores = (
        jnp.einsum("rhk,rlk->rhl", query_lat, kv_cache, preferred_element_type=jnp.float32)
        * score_scale
    )
    positions = jnp.arange(kv_cache.shape[1], dtype=jnp.int32)
    visible = positions[None, None, :] < cache_len[:, None, None]
    scores = jnp.where(visible, scores, jnp.float32(-1e30))
    top_score = jnp.max(scores, axis=2, keepdims=True)
    exponent = jnp.exp(scores - top_score)
    denominator = jnp.sum(exponent, axis=2, keepdims=True)
    weights = (exponent / denominator).astype(jnp.bfloat16)
    return jnp.einsum(
        "rhl,rlc->rhc", weights, kv_cache[:, :, :LAT], preferred_element_type=jnp.float32
    ).astype(jnp.bfloat16)


def routing_tables(expert_ids, gate_coef, expert_count, capacity):
    row_count, top_count = expert_ids.shape
    flat_ids = expert_ids.reshape(-1)
    position_ids = jnp.arange(flat_ids.shape[0], dtype=jnp.int32)
    matches = (flat_ids[:, None] == flat_ids[None, :]) & (
        position_ids[None, :] < position_ids[:, None]
    )
    slot_rank = jnp.sum(matches.astype(jnp.int32), axis=1)
    target = flat_ids * capacity + slot_rank
    slot_ids = jnp.arange(expert_count * capacity, dtype=jnp.int32)
    placed = (target[None, :] == slot_ids[:, None]).astype(jnp.float32)
    owner_hot = (
        (position_ids // top_count)[:, None] == jnp.arange(row_count, dtype=jnp.int32)[None, :]
    ).astype(jnp.float32)
    picker = jnp.dot(placed, owner_hot, precision=lax.Precision.HIGHEST).astype(jnp.bfloat16)
    weighted = owner_hot * gate_coef.reshape(-1)[:, None]
    mixing = jnp.dot(weighted.T, placed.T, precision=lax.Precision.HIGHEST)
    return (picker, mixing)


def expert_rows(tokens, gate_weight, up_weight, down_weight):
    shape_in = tokens.shape
    flat_rows = tokens.reshape(-1, shape_in[-1])
    gate_val = jnp.dot(flat_rows, gate_weight[0], preferred_element_type=jnp.float32)
    up_val = jnp.dot(flat_rows, up_weight[0], preferred_element_type=jnp.float32)
    hidden = (jax.nn.silu(gate_val) * up_val).astype(jnp.bfloat16)
    part_out = jnp.dot(hidden, down_weight[0], preferred_element_type=jnp.float32).astype(
        jnp.bfloat16
    )
    return part_out.reshape(shape_in)


def route_tokens(send_buf, gate_weight, up_weight, down_weight):
    section_count = lax.axis_size("sec")
    doubled = jnp.concatenate([send_buf] * section_count, axis=0)
    halves = expert_rows(
        lax.all_to_all(doubled, AXES, split_axis=0, concat_axis=0, tiled=True),
        gate_weight,
        up_weight,
        down_weight,
    )
    returned = lax.all_to_all(halves, AXES, split_axis=0, concat_axis=0, tiled=True)
    pieces = returned.reshape((section_count,) + send_buf.shape).astype(jnp.float32)
    return jnp.sum(pieces, axis=0).astype(jnp.bfloat16)


def combine(returned, mixing):
    flat_back = returned.reshape(-1, returned.shape[-1]).astype(jnp.float32)
    return jnp.dot(mixing, flat_back, precision=lax.Precision.HIGHEST).astype(jnp.bfloat16)


def routed_sparse(
    hidden_in, expert_ids, gate_coef, gate_weight, up_weight, down_weight, half_rows, capacity
):
    model_width = hidden_in.shape[1]
    expert_count = lax.axis_size("dev")
    outs = []
    for offset in (0, half_rows):
        picker, mixing = routing_tables(
            expert_ids[offset : offset + half_rows],
            gate_coef[offset : offset + half_rows],
            expert_count,
            capacity,
        )
        gathered = jnp.dot(
            picker, hidden_in[offset : offset + half_rows], preferred_element_type=jnp.float32
        ).astype(jnp.bfloat16)
        send_buf = gathered.reshape(expert_count, capacity, model_width)
        outs.append(combine(route_tokens(send_buf, gate_weight, up_weight, down_weight), mixing))
    return jnp.concatenate(outs, axis=0)


def permutation(n_dev, move):
    pairs = []
    for y in range(2):
        for d in range(n_dev):
            there = move(y, d // 4, (d // 2) % 2, d % 2)
            if there is not None:
                ty, tz, tx, tc = there
                pairs.append((y * n_dev + d, ty * n_dev + tz * 4 + tx * 2 + tc))
    return lambda a: lax.ppermute(a, AXES, pairs)


class Moves:
    def __init__(self, n_dev):
        line = n_dev // 4
        self.line = line
        self.core = permutation(n_dev, lambda y, z, x, c: (y, z, x, 1 - c))
        self.first = permutation(
            n_dev, lambda y, z, x, c: (1 - y, z, x, c) if c else (y, z, 1 - x, c)
        )
        self.second = permutation(
            n_dev, lambda y, z, x, c: (y, z, 1 - x, c) if c else (1 - y, z, x, c)
        )
        self.ring = permutation(n_dev, lambda y, z, x, c: (y, (z + 1) % line, x, c))


def plus(*terms):
    total = terms[0].astype(jnp.float32)
    for t in terms[1:]:
        total = total + t.astype(jnp.float32)
    return total.astype(jnp.bfloat16)


def plane_gather(mv, block):
    near = jnp.concatenate([block, mv.first(block)], axis=0)
    far = mv.second(near)
    return [near, far, mv.core(near), mv.core(far)]


def plane_sum(mv, y, *more):
    near, far, other_near, other_far = y
    half = near.shape[0] // 2
    crossed = mv.second(plus(far, mv.core(other_far)))
    other = mv.core(other_near)
    side = plus(near[half:], other[half:], crossed[half:])
    return plus(near[:half], other[:half], crossed[:half], mv.first(side), *more)


def spread_coefs(expert_ids, gate_coef, expert_count):
    hot = expert_ids[:, :, None] == jnp.arange(expert_count, dtype=jnp.int32)[None, None, :]
    dense = jnp.sum(jnp.where(hot, gate_coef[:, :, None], 0.0), axis=1)
    high = lax.reduce_precision(dense, 8, 7)
    parts = jnp.concatenate([high, dense - high], axis=1).astype(jnp.bfloat16)
    pad = -parts.shape[1] % 128
    return jnp.pad(parts, ((0, 0), (0, pad)))


def expert_kernel(n_x, n_experts, steps, me, w_gate, w_up, w_down, *refs):
    xs, outs = refs[:n_x], refs[n_x : 2 * n_x]
    x, acc_gate, acc_up, hidden, coef, y, x_sem, y_sem = refs[2 * n_x :]
    rows = xs[0].shape[0]
    width = w_gate.shape[1]
    chunk = width // steps
    part = [pl.ds(k * chunk, chunk) for k in range(steps)]
    group = [pl.ds(j * rows, rows) for j in range(n_x)]
    x_in = [pltpu.make_async_copy(xs[j], x.at[group[j]], x_sem) for j in range(n_x)]
    for c in x_in:
        c.start()
    for c in x_in:
        c.wait()
    tail = x[:, width:].astype(jnp.float32)
    lane = lax.broadcasted_iota(jnp.int32, tail.shape, 1)
    mine = (lane == me[0]) | (lane == me[0] + n_experts)
    picked = jnp.sum(jnp.where(mine, tail, 0.0), axis=1, keepdims=True)
    coef[...] = jnp.broadcast_to(picked, coef.shape)
    for k in range(steps):
        xk = x[:, part[k]]
        g = jnp.dot(xk, w_gate[0, part[k], :], preferred_element_type=jnp.float32)
        u = jnp.dot(xk, w_up[0, part[k], :], preferred_element_type=jnp.float32)
        if k == 0:
            acc_gate[...] = g
            acc_up[...] = u
        else:
            acc_gate[...] += g
            acc_up[...] += u
    g = acc_gate[...]
    hidden[...] = (g / (1.0 + jnp.exp(-g)) * acc_up[...]).astype(jnp.bfloat16)
    y_out = []
    for k in range(steps):
        yk = jnp.dot(hidden[...], w_down[0, :, part[k]], preferred_element_type=jnp.float32)
        y[:, part[k]] = (yk * coef[:, :1]).astype(jnp.bfloat16)
        for j in range(n_x):
            c = pltpu.make_async_copy(y.at[group[j], part[k]], outs[j].at[:, part[k]], y_sem)
            c.start()
            y_out.append(c)
    for c in y_out:
        c.wait()


def expert_group(xs, gate_weight, up_weight, down_weight, n_experts):
    rows, total = xs[0].shape
    _, width, hidden_width = gate_weight.shape
    chunk = max(c for c in range(128, 1025, 128) if width % c == 0)
    steps = width // chunk
    n_x = len(xs)
    m = n_x * rows
    me = lax.axis_index("dev").astype(jnp.int32).reshape(1)
    anywhere = pl.BlockSpec(memory_space=pl.ANY)
    held = pl.BlockSpec(memory_space=pltpu.VMEM)
    return pl.pallas_call(
        functools.partial(expert_kernel, n_x, n_experts, steps),
        in_specs=[pl.BlockSpec(memory_space=pltpu.SMEM)] + [held] * 3 + [anywhere] * n_x,
        out_specs=[anywhere] * n_x,
        scratch_shapes=[
            pltpu.VMEM((m, total), jnp.bfloat16),
            pltpu.VMEM((m, hidden_width), jnp.float32),
            pltpu.VMEM((m, hidden_width), jnp.float32),
            pltpu.VMEM((m, hidden_width), jnp.bfloat16),
            pltpu.VMEM((m, 128), jnp.float32),
            pltpu.VMEM((m, width), jnp.bfloat16),
            pltpu.SemaphoreType.DMA,
            pltpu.SemaphoreType.DMA,
        ],
        out_shape=[jax.ShapeDtypeStruct((rows, width), jnp.bfloat16)] * n_x,
        compiler_params=pltpu.CompilerParams(vmem_limit_bytes=14 * 2**20),
        cost_estimate=pl.CostEstimate(
            flops=6 * m * width * hidden_width,
            bytes_accessed=6 * width * hidden_width + 4 * m * width,
            transcendentals=m * hidden_width,
        ),
        name="experts",
    )(me, gate_weight, up_weight, down_weight, *xs)


def routed_dense(hidden_in, expert_ids, gate_coef, gate_weight, up_weight, down_weight):
    n_dev = lax.axis_size("dev")
    mv = Moves(n_dev)
    coefs = spread_coefs(expert_ids, gate_coef, n_dev)
    blocks = [jnp.concatenate([hidden_in, coefs], axis=1)]
    for _ in range(mv.line - 1):
        blocks.append(mv.ring(blocks[-1]))
    gathered = [plane_gather(mv, b) for b in blocks]
    half = mv.line // 2
    sums = []
    for group in (gathered[:half], gathered[half:]):
        ys = expert_group(sum(group, []), gate_weight, up_weight, down_weight, n_dev)
        sums += [ys[4 * k : 4 * k + 4] for k in range(len(group))]
    acc = None
    for y in sums[1:]:
        acc = mv.ring(plane_sum(mv, y) if acc is None else plane_sum(mv, y, acc))
    return plane_sum(mv, sums[0], acc)


def per_device(
    hidden_in,
    expert_ids,
    gate_coef,
    query_lat,
    kv_cache,
    cache_len,
    gate_weight,
    up_weight,
    down_weight,
):
    half_rows = hidden_in.shape[0] // 2
    expert_count = lax.axis_size("dev")
    capacity = max(2, 2 * TOP * half_rows // expert_count)
    weights = (gate_weight, up_weight, down_weight)
    if capacity < half_rows:
        routed_out = routed_sparse(
            hidden_in, expert_ids, gate_coef, *weights, half_rows, capacity
        )
    else:
        routed_out = routed_dense(hidden_in, expert_ids, gate_coef, *weights)
    attention = attend(query_lat, kv_cache, cache_len)
    return (attention, routed_out)


def solution(mesh):
    in_specs = (
        P(("sec", "dev"), None),
        P(("sec", "dev"), None),
        P(("sec", "dev"), None),
        P(("sec", "dev"), None, None),
        P(("sec", "dev"), None, None),
        P(("sec", "dev")),
        P("dev", None, "sec"),
        P("dev", None, "sec"),
        P("dev", "sec", None),
    )
    out_specs = (P(("sec", "dev"), None, None), P(("sec", "dev"), None))
    return jax.shard_map(
        per_device, mesh=mesh, in_specs=in_specs, out_specs=out_specs, check_vma=False
    )
```

```python
import functools
import math

import jax
import jax.numpy as jnp
from jax import lax
from jax.experimental import pallas as pl
from jax.experimental.pallas import tpu as pltpu
from jax.sharding import PartitionSpec as P

LAT = 512
TOP = 8
AXES = ("sec", "dev")

score_scale = 1.0 / math.sqrt(192.0)


def attend(query_lat, kv_cache, cache_len):
    scores = (
        jnp.einsum("rhk,rlk->rhl", query_lat, kv_cache, preferred_element_type=jnp.float32)
        * score_scale
    )
    positions = jnp.arange(kv_cache.shape[1], dtype=jnp.int32)
    visible = positions[None, None, :] < cache_len[:, None, None]
    scores = jnp.where(visible, scores, jnp.float32(-1e30))
    top_score = jnp.max(scores, axis=2, keepdims=True)
    exponent = jnp.exp(scores - top_score)
    denominator = jnp.sum(exponent, axis=2, keepdims=True)
    weights = (exponent / denominator).astype(jnp.bfloat16)
    return jnp.einsum(
        "rhl,rlc->rhc", weights, kv_cache[:, :, :LAT], preferred_element_type=jnp.float32
    ).astype(jnp.bfloat16)


def routing_tables(expert_ids, gate_coef, expert_count, capacity):
    row_count, top_count = expert_ids.shape
    flat_ids = expert_ids.reshape(-1)
    position_ids = jnp.arange(flat_ids.shape[0], dtype=jnp.int32)
    matches = (flat_ids[:, None] == flat_ids[None, :]) & (
        position_ids[None, :] < position_ids[:, None]
    )
    slot_rank = jnp.sum(matches.astype(jnp.int32), axis=1)
    target = flat_ids * capacity + slot_rank
    slot_ids = jnp.arange(expert_count * capacity, dtype=jnp.int32)
    placed = (target[None, :] == slot_ids[:, None]).astype(jnp.float32)
    owner_hot = (
        (position_ids // top_count)[:, None] == jnp.arange(row_count, dtype=jnp.int32)[None, :]
    ).astype(jnp.float32)
    picker = jnp.dot(placed, owner_hot, precision=lax.Precision.HIGHEST).astype(jnp.bfloat16)
    weighted = owner_hot * gate_coef.reshape(-1)[:, None]
    mixing = jnp.dot(weighted.T, placed.T, precision=lax.Precision.HIGHEST)
    return (picker, mixing)


def expert_rows(tokens, gate_weight, up_weight, down_weight):
    shape_in = tokens.shape
    flat_rows = tokens.reshape(-1, shape_in[-1])
    gate_val = jnp.dot(flat_rows, gate_weight[0], preferred_element_type=jnp.float32)
    up_val = jnp.dot(flat_rows, up_weight[0], preferred_element_type=jnp.float32)
    hidden = (jax.nn.silu(gate_val) * up_val).astype(jnp.bfloat16)
    part_out = jnp.dot(hidden, down_weight[0], preferred_element_type=jnp.float32).astype(
        jnp.bfloat16
    )
    return part_out.reshape(shape_in)


def route_tokens(send_buf, gate_weight, up_weight, down_weight):
    section_count = lax.axis_size("sec")
    doubled = jnp.concatenate([send_buf] * section_count, axis=0)
    halves = expert_rows(
        lax.all_to_all(doubled, AXES, split_axis=0, concat_axis=0, tiled=True),
        gate_weight,
        up_weight,
        down_weight,
    )
    returned = lax.all_to_all(halves, AXES, split_axis=0, concat_axis=0, tiled=True)
    pieces = returned.reshape((section_count,) + send_buf.shape).astype(jnp.float32)
    return jnp.sum(pieces, axis=0).astype(jnp.bfloat16)


def combine(returned, mixing):
    flat_back = returned.reshape(-1, returned.shape[-1]).astype(jnp.float32)
    return jnp.dot(mixing, flat_back, precision=lax.Precision.HIGHEST).astype(jnp.bfloat16)


def routed_sparse(
    hidden_in, expert_ids, gate_coef, gate_weight, up_weight, down_weight, half_rows, capacity
):
    model_width = hidden_in.shape[1]
    expert_count = lax.axis_size("dev")
    outs = []
    for offset in (0, half_rows):
        picker, mixing = routing_tables(
            expert_ids[offset : offset + half_rows],
            gate_coef[offset : offset + half_rows],
            expert_count,
            capacity,
        )
        gathered = jnp.dot(
            picker, hidden_in[offset : offset + half_rows], preferred_element_type=jnp.float32
        ).astype(jnp.bfloat16)
        send_buf = gathered.reshape(expert_count, capacity, model_width)
        outs.append(combine(route_tokens(send_buf, gate_weight, up_weight, down_weight), mixing))
    return jnp.concatenate(outs, axis=0)


def permutation(n_dev, move):
    pairs = []
    for y in range(2):
        for d in range(n_dev):
            there = move(y, d // 4, (d // 2) % 2, d % 2)
            if there is not None:
                ty, tz, tx, tc = there
                pairs.append((y * n_dev + d, ty * n_dev + tz * 4 + tx * 2 + tc))
    return lambda a: lax.ppermute(a, AXES, pairs)


class Moves:
    def __init__(self, n_dev):
        line = n_dev // 4
        self.line = line
        self.core = permutation(n_dev, lambda y, z, x, c: (y, z, x, 1 - c))
        self.first = permutation(
            n_dev, lambda y, z, x, c: (1 - y, z, x, c) if c else (y, z, 1 - x, c)
        )
        self.second = permutation(
            n_dev, lambda y, z, x, c: (y, z, 1 - x, c) if c else (1 - y, z, x, c)
        )
        self.ring = permutation(n_dev, lambda y, z, x, c: (y, (z + 1) % line, x, c))


def plus(*terms):
    total = terms[0].astype(jnp.float32)
    for t in terms[1:]:
        total = total + t.astype(jnp.float32)
    return total.astype(jnp.bfloat16)


ANYWHERE = pl.BlockSpec(memory_space=pl.ANY)
FAR = pl.BlockSpec(memory_space=pltpu.HBM)
HELD = pl.BlockSpec(memory_space=pltpu.VMEM)
SCALARS = pl.BlockSpec(memory_space=pltpu.SMEM)


def pack_kernel(n_experts, ids, coefs, x, out):
    rows, width = x.shape
    hot = lax.broadcasted_iota(jnp.int32, (n_experts, rows), 0)
    dense = jnp.zeros((n_experts, rows), jnp.float32)
    for k in range(ids.shape[0]):
        dense += jnp.where(hot == ids[k : k + 1, :], coefs[k : k + 1, :], 0.0)
    high = dense.astype(jnp.bfloat16)
    low = (dense - high.astype(jnp.float32)).astype(jnp.bfloat16)
    rest = jnp.zeros((out.shape[1] - width - 2 * n_experts, rows), jnp.bfloat16)
    parts = jnp.concatenate([high, low, rest], axis=0)
    same = lax.broadcasted_iota(jnp.int32, (rows, rows), 0) == lax.broadcasted_iota(
        jnp.int32, (rows, rows), 1
    )
    turned = lax.dot_general(
        same.astype(jnp.bfloat16),
        parts,
        (((1,), (1,)), ((), ())),
        preferred_element_type=jnp.float32,
    )
    out[:, :width] = x[...]
    out[:, width:] = turned.astype(jnp.bfloat16)


def pack_rows(hidden_in, expert_ids, gate_coef, n_experts):
    rows, width = hidden_in.shape
    tail = 2 * n_experts + -2 * n_experts % 128
    return pl.pallas_call(
        functools.partial(pack_kernel, n_experts),
        in_specs=[HELD] * 3,
        out_specs=HELD,
        out_shape=jax.ShapeDtypeStruct((rows, width + tail), jnp.bfloat16),
        name="pack",
    )(expert_ids.T, gate_coef.T, hidden_in)


def expert_kernel(sizes, sizes_out, n_experts, steps, me, gate, up, down, *refs):
    xs = refs[: len(sizes)]
    outs = refs[-10 - len(sizes_out) : -10]
    w_gate, w_up, w_down, acc_gate, acc_up, hidden, coef = refs[-10:-3]
    gate_sem, up_sem, down_sem = refs[-3:]
    width = w_gate.shape[0]
    chunk = width // steps
    copy = pltpu.make_async_copy
    part = [pl.ds(k * chunk, chunk) for k in range(steps)]
    gate_in = [copy(gate.at[0, p], w_gate.at[p], gate_sem.at[k]) for k, p in enumerate(part)]
    up_in = [copy(up.at[0, p], w_up.at[p], up_sem.at[k]) for k, p in enumerate(part)]
    down_in = [copy(down.at[0, :, p], w_down.at[:, p], down_sem.at[k]) for k, p in enumerate(part)]
    for k in range(steps):
        gate_in[k].start()
        up_in[k].start()
    for c in down_in:
        c.start()
    tail = jnp.concatenate([x[:, width:] for x in xs], axis=0).astype(jnp.float32)
    lane = lax.broadcasted_iota(jnp.int32, tail.shape, 1)
    mine = (lane == me[0]) | (lane == me[0] + n_experts)
    picked = jnp.sum(jnp.where(mine, tail, 0.0), axis=1, keepdims=True)
    coef[...] = jnp.broadcast_to(picked, coef.shape)
    for k in range(steps):
        gate_in[k].wait()
        up_in[k].wait()
        xk = jnp.concatenate([x[:, part[k]] for x in xs], axis=0)
        g = jnp.dot(xk, w_gate[part[k], :], preferred_element_type=jnp.float32)
        u = jnp.dot(xk, w_up[part[k], :], preferred_element_type=jnp.float32)
        if k == 0:
            acc_gate[...] = g
            acc_up[...] = u
        else:
            acc_gate[...] += g
            acc_up[...] += u
    g = acc_gate[...]
    hidden[...] = (g / (1.0 + jnp.exp(-g)) * acc_up[...]).astype(jnp.bfloat16)
    for k in range(steps):
        down_in[k].wait()
        yk = jnp.dot(hidden[...], w_down[:, part[k]], preferred_element_type=jnp.float32)
        yk = (yk * coef[:, :1]).astype(jnp.bfloat16)
        row = 0
        for out in outs:
            out[:, part[k]] = yk[row : row + out.shape[0]]
            row += out.shape[0]


def expert_group(xs, slots, gate_weight, up_weight, down_weight, n_experts, *after):
    sizes = [x.shape[0] for x in xs]
    m = sum(sizes)
    _, width, hidden_width = gate_weight.shape
    chunk = max(c for c in range(128, 1025, 128) if width % c == 0)
    steps = width // chunk
    quarter = m // slots // 4
    outs = [quarter] * (2 * slots) + [2 * quarter] * slots
    me = lax.axis_index("dev").astype(jnp.int32).reshape(1)
    return pl.pallas_call(
        functools.partial(expert_kernel, sizes, outs, n_experts, steps),
        in_specs=[SCALARS] + [FAR] * 3 + [HELD] * len(xs) + [ANYWHERE] * len(after),
        out_specs=[HELD] * len(outs),
        scratch_shapes=[
            pltpu.VMEM((width, hidden_width), jnp.bfloat16),
            pltpu.VMEM((width, hidden_width), jnp.bfloat16),
            pltpu.VMEM((hidden_width, width), jnp.bfloat16),
            pltpu.VMEM((m, hidden_width), jnp.float32),
            pltpu.VMEM((m, hidden_width), jnp.float32),
            pltpu.VMEM((m, hidden_width), jnp.bfloat16),
            pltpu.VMEM((m, 128), jnp.float32),
            pltpu.SemaphoreType.DMA((steps,)),
            pltpu.SemaphoreType.DMA((steps,)),
            pltpu.SemaphoreType.DMA((steps,)),
        ],
        out_shape=[jax.ShapeDtypeStruct((r, width), jnp.bfloat16) for r in outs],
        compiler_params=pltpu.CompilerParams(vmem_limit_bytes=28 * 2**20),
        cost_estimate=pl.CostEstimate(
            flops=6 * m * width * hidden_width,
            bytes_accessed=1,
            transcendentals=m * hidden_width,
        ),
        name="experts",
    )(me, gate_weight, up_weight, down_weight, *xs, *after)


def routed_dense(hidden_in, expert_ids, gate_coef, gate_weight, up_weight, down_weight):
    n_dev = lax.axis_size("dev")
    mv = Moves(n_dev)
    weights = (gate_weight, up_weight, down_weight)
    n = mv.line
    half = n // 2
    cat = lambda *a: jnp.concatenate(a, axis=0)
    block = [pack_rows(hidden_in, expert_ids, gate_coef, n_dev)]
    for _ in range(n - 1):
        block.append(mv.ring(block[-1]))
    near = [cat(b, mv.first(b)) for b in block]
    far = [mv.second(a) for a in near]
    pairs = [a for k in range(n) for a in (near[k], far[k])]
    own = cat(*pairs[: 2 * half])
    early = expert_group([own, mv.core(own)], half, *weights, n_dev)
    late = []
    for k in range(half, n - 1):
        late.append(cat(near[k], far[k]))
    late += pairs[2 * n - 2 :]
    late = expert_group(late + [mv.core(a) for a in late], n - half, *weights, n_dev, early[0])
    y_near = early[0 : 2 * half : 2] + late[0 : 2 * (n - half) : 2]
    y_far = early[1 : 2 * half : 2] + late[1 : 2 * (n - half) : 2]
    mine = [mv.core(a) for a in early[2 * half :] + late[2 * (n - half) :]]
    rows = block[0].shape[0]
    acc = ()
    for k in list(range(1, n)) + [0]:
        crossed = mv.second(plus(y_far[k], mine[k][2 * rows :]))
        side = mv.first(plus(y_near[k][rows:], mine[k][rows : 2 * rows], crossed[rows:]))
        total = plus(y_near[k][:rows], mine[k][:rows], crossed[:rows], side, *acc)
        if k:
            acc = (mv.ring(total),)
    return total


def per_device(
    hidden_in,
    expert_ids,
    gate_coef,
    query_lat,
    kv_cache,
    cache_len,
    gate_weight,
    up_weight,
    down_weight,
):
    half_rows = hidden_in.shape[0] // 2
    expert_count = lax.axis_size("dev")
    capacity = max(2, 2 * TOP * half_rows // expert_count)
    weights = (gate_weight, up_weight, down_weight)
    if capacity < half_rows:
        routed_out = routed_sparse(
            hidden_in, expert_ids, gate_coef, *weights, half_rows, capacity
        )
    else:
        routed_out = routed_dense(hidden_in, expert_ids, gate_coef, *weights)
    attention = attend(query_lat, kv_cache, cache_len)
    return (attention, routed_out)


def solution(mesh):
    in_specs = (
        P(("sec", "dev"), None),
        P(("sec", "dev"), None),
        P(("sec", "dev"), None),
        P(("sec", "dev"), None, None),
        P(("sec", "dev"), None, None),
        P(("sec", "dev")),
        P("dev", None, "sec"),
        P("dev", None, "sec"),
        P("dev", "sec", None),
    )
    out_specs = (P(("sec", "dev"), None, None), P(("sec", "dev"), None))
    return jax.shard_map(
        per_device, mesh=mesh, in_specs=in_specs, out_specs=out_specs, check_vma=False
    )
```

```python
import functools
import math

import jax
import jax.numpy as jnp
from jax import lax
from jax.experimental import pallas as pl
from jax.experimental.pallas import tpu as pltpu
from jax.sharding import PartitionSpec as P

LAT = 512
TOP = 8
AXES = ("sec", "dev")

score_scale = 1.0 / math.sqrt(192.0)


def attend(query_lat, kv_cache, cache_len):
    scores = (
        jnp.einsum("rhk,rlk->rhl", query_lat, kv_cache, preferred_element_type=jnp.float32)
        * score_scale
    )
    positions = jnp.arange(kv_cache.shape[1], dtype=jnp.int32)
    visible = positions[None, None, :] < cache_len[:, None, None]
    scores = jnp.where(visible, scores, jnp.float32(-1e30))
    top_score = jnp.max(scores, axis=2, keepdims=True)
    exponent = jnp.exp(scores - top_score)
    denominator = jnp.sum(exponent, axis=2, keepdims=True)
    weights = (exponent / denominator).astype(jnp.bfloat16)
    return jnp.einsum(
        "rhl,rlc->rhc", weights, kv_cache[:, :, :LAT], preferred_element_type=jnp.float32
    ).astype(jnp.bfloat16)


def routing_tables(expert_ids, gate_coef, expert_count, capacity):
    row_count, top_count = expert_ids.shape
    flat_ids = expert_ids.reshape(-1)
    position_ids = jnp.arange(flat_ids.shape[0], dtype=jnp.int32)
    matches = (flat_ids[:, None] == flat_ids[None, :]) & (
        position_ids[None, :] < position_ids[:, None]
    )
    slot_rank = jnp.sum(matches.astype(jnp.int32), axis=1)
    target = flat_ids * capacity + slot_rank
    slot_ids = jnp.arange(expert_count * capacity, dtype=jnp.int32)
    placed = (target[None, :] == slot_ids[:, None]).astype(jnp.float32)
    owner_hot = (
        (position_ids // top_count)[:, None] == jnp.arange(row_count, dtype=jnp.int32)[None, :]
    ).astype(jnp.float32)
    picker = jnp.dot(placed, owner_hot, precision=lax.Precision.HIGHEST).astype(jnp.bfloat16)
    weighted = owner_hot * gate_coef.reshape(-1)[:, None]
    mixing = jnp.dot(weighted.T, placed.T, precision=lax.Precision.HIGHEST)
    return (picker, mixing)


def expert_rows(tokens, gate_weight, up_weight, down_weight):
    shape_in = tokens.shape
    flat_rows = tokens.reshape(-1, shape_in[-1])
    gate_val = jnp.dot(flat_rows, gate_weight[0], preferred_element_type=jnp.float32)
    up_val = jnp.dot(flat_rows, up_weight[0], preferred_element_type=jnp.float32)
    hidden = (jax.nn.silu(gate_val) * up_val).astype(jnp.bfloat16)
    part_out = jnp.dot(hidden, down_weight[0], preferred_element_type=jnp.float32).astype(
        jnp.bfloat16
    )
    return part_out.reshape(shape_in)


def route_tokens(send_buf, gate_weight, up_weight, down_weight):
    section_count = lax.axis_size("sec")
    doubled = jnp.concatenate([send_buf] * section_count, axis=0)
    halves = expert_rows(
        lax.all_to_all(doubled, AXES, split_axis=0, concat_axis=0, tiled=True),
        gate_weight,
        up_weight,
        down_weight,
    )
    returned = lax.all_to_all(halves, AXES, split_axis=0, concat_axis=0, tiled=True)
    pieces = returned.reshape((section_count,) + send_buf.shape).astype(jnp.float32)
    return jnp.sum(pieces, axis=0).astype(jnp.bfloat16)


def combine(returned, mixing):
    flat_back = returned.reshape(-1, returned.shape[-1]).astype(jnp.float32)
    return jnp.dot(mixing, flat_back, precision=lax.Precision.HIGHEST).astype(jnp.bfloat16)


def routed_sparse(
    hidden_in, expert_ids, gate_coef, gate_weight, up_weight, down_weight, half_rows, capacity
):
    model_width = hidden_in.shape[1]
    expert_count = lax.axis_size("dev")
    outs = []
    for offset in (0, half_rows):
        picker, mixing = routing_tables(
            expert_ids[offset : offset + half_rows],
            gate_coef[offset : offset + half_rows],
            expert_count,
            capacity,
        )
        gathered = jnp.dot(
            picker, hidden_in[offset : offset + half_rows], preferred_element_type=jnp.float32
        ).astype(jnp.bfloat16)
        send_buf = gathered.reshape(expert_count, capacity, model_width)
        outs.append(combine(route_tokens(send_buf, gate_weight, up_weight, down_weight), mixing))
    return jnp.concatenate(outs, axis=0)


def permutation(n_dev, move):
    pairs = []
    for y in range(2):
        for d in range(n_dev):
            there = move(y, d // 4, (d // 2) % 2, d % 2)
            if there is not None:
                ty, tz, tx, tc = there
                pairs.append((y * n_dev + d, ty * n_dev + tz * 4 + tx * 2 + tc))
    return lambda a: lax.ppermute(a, AXES, pairs)


class Moves:
    def __init__(self, n_dev):
        line = n_dev // 4
        self.line = line
        self.core = permutation(n_dev, lambda y, z, x, c: (y, z, x, 1 - c))
        self.first = permutation(
            n_dev, lambda y, z, x, c: (1 - y, z, x, c) if c else (y, z, 1 - x, c)
        )
        self.second = permutation(
            n_dev, lambda y, z, x, c: (y, z, 1 - x, c) if c else (1 - y, z, x, c)
        )
        self.ring = permutation(n_dev, lambda y, z, x, c: (y, (z + 1) % line, x, c))


def plus(*terms):
    total = terms[0].astype(jnp.float32)
    for t in terms[1:]:
        total = total + t.astype(jnp.float32)
    return total.astype(jnp.bfloat16)


def after(a, other):
    return a + other[:1, :1] * 0


ANYWHERE = pl.BlockSpec(memory_space=pl.ANY)
FAR = pl.BlockSpec(memory_space=pltpu.HBM)
HELD = pl.BlockSpec(memory_space=pltpu.VMEM)
SCALARS = pl.BlockSpec(memory_space=pltpu.SMEM)


def pack_kernel(n_experts, ids, coefs, x, out):
    rows, width = x.shape
    hot = lax.broadcasted_iota(jnp.int32, (n_experts, rows), 0)
    dense = jnp.zeros((n_experts, rows), jnp.float32)
    for k in range(ids.shape[0]):
        dense += jnp.where(hot == ids[k : k + 1, :], coefs[k : k + 1, :], 0.0)
    high = dense.astype(jnp.bfloat16)
    low = (dense - high.astype(jnp.float32)).astype(jnp.bfloat16)
    rest = jnp.zeros((out.shape[1] - width - 2 * n_experts, rows), jnp.bfloat16)
    parts = jnp.concatenate([high, low, rest], axis=0)
    same = lax.broadcasted_iota(jnp.int32, (rows, rows), 0) == lax.broadcasted_iota(
        jnp.int32, (rows, rows), 1
    )
    turned = lax.dot_general(
        same.astype(jnp.bfloat16),
        parts,
        (((1,), (1,)), ((), ())),
        preferred_element_type=jnp.float32,
    )
    out[:, :width] = x[...]
    out[:, width:] = turned.astype(jnp.bfloat16)


def pack_rows(hidden_in, expert_ids, gate_coef, n_experts):
    rows, width = hidden_in.shape
    tail = 2 * n_experts + -2 * n_experts % 128
    return pl.pallas_call(
        functools.partial(pack_kernel, n_experts),
        in_specs=[HELD] * 3,
        out_specs=HELD,
        out_shape=jax.ShapeDtypeStruct((rows, width + tail), jnp.bfloat16),
        name="pack",
    )(expert_ids.T, gate_coef.T, hidden_in)


def expert_kernel(sizes, sizes_out, n_experts, steps, me, gate, up, down, *refs):
    xs = refs[: len(sizes)]
    outs = refs[-10 - len(sizes_out) : -10]
    w_gate, w_up, w_down, acc_gate, acc_up, hidden, coef = refs[-10:-3]
    gate_sem, up_sem, down_sem = refs[-3:]
    width = w_gate.shape[0]
    chunk = width // steps
    copy = pltpu.make_async_copy
    part = [pl.ds(k * chunk, chunk) for k in range(steps)]
    gate_in = [copy(gate.at[0, p], w_gate.at[p], gate_sem.at[k]) for k, p in enumerate(part)]
    up_in = [copy(up.at[0, p], w_up.at[p], up_sem.at[k]) for k, p in enumerate(part)]
    down_in = [copy(down.at[0, :, p], w_down.at[:, p], down_sem.at[k]) for k, p in enumerate(part)]
    for k in range(steps):
        gate_in[k].start()
        up_in[k].start()
    for c in down_in:
        c.start()
    tail = jnp.concatenate([x[:, width:] for x in xs], axis=0).astype(jnp.float32)
    lane = lax.broadcasted_iota(jnp.int32, tail.shape, 1)
    mine = (lane == me[0]) | (lane == me[0] + n_experts)
    picked = jnp.sum(jnp.where(mine, tail, 0.0), axis=1, keepdims=True)
    coef[...] = jnp.broadcast_to(picked, coef.shape)
    for k in range(steps):
        gate_in[k].wait()
        up_in[k].wait()
        xk = jnp.concatenate([x[:, part[k]] for x in xs], axis=0)
        g = jnp.dot(xk, w_gate[part[k], :], preferred_element_type=jnp.float32)
        u = jnp.dot(xk, w_up[part[k], :], preferred_element_type=jnp.float32)
        if k == 0:
            acc_gate[...] = g
            acc_up[...] = u
        else:
            acc_gate[...] += g
            acc_up[...] += u
    g = acc_gate[...]
    hidden[...] = (g / (1.0 + jnp.exp(-g)) * acc_up[...]).astype(jnp.bfloat16)
    for k in range(steps):
        down_in[k].wait()
        yk = jnp.dot(hidden[...], w_down[:, part[k]], preferred_element_type=jnp.float32)
        yk = (yk * coef[:, :1]).astype(jnp.bfloat16)
        row = 0
        for out in outs:
            out[:, part[k]] = yk[row : row + out.shape[0]]
            row += out.shape[0]


def expert_group(xs, slots, gate_weight, up_weight, down_weight, n_experts, *after):
    sizes = [x.shape[0] for x in xs]
    m = sum(sizes)
    _, width, hidden_width = gate_weight.shape
    chunk = max(c for c in range(128, 1025, 128) if width % c == 0)
    steps = width // chunk
    quarter = m // slots // 4
    outs = [quarter] * (2 * slots) + [2 * quarter] * slots
    me = lax.axis_index("dev").astype(jnp.int32).reshape(1)
    return pl.pallas_call(
        functools.partial(expert_kernel, sizes, outs, n_experts, steps),
        in_specs=[SCALARS] + [FAR] * 3 + [HELD] * len(xs) + [ANYWHERE] * len(after),
        out_specs=[HELD] * len(outs),
        scratch_shapes=[
            pltpu.VMEM((width, hidden_width), jnp.bfloat16),
            pltpu.VMEM((width, hidden_width), jnp.bfloat16),
            pltpu.VMEM((hidden_width, width), jnp.bfloat16),
            pltpu.VMEM((m, hidden_width), jnp.float32),
            pltpu.VMEM((m, hidden_width), jnp.float32),
            pltpu.VMEM((m, hidden_width), jnp.bfloat16),
            pltpu.VMEM((m, 128), jnp.float32),
            pltpu.SemaphoreType.DMA((steps,)),
            pltpu.SemaphoreType.DMA((steps,)),
            pltpu.SemaphoreType.DMA((steps,)),
        ],
        out_shape=[jax.ShapeDtypeStruct((r, width), jnp.bfloat16) for r in outs],
        compiler_params=pltpu.CompilerParams(vmem_limit_bytes=33 * 2**20),
        cost_estimate=pl.CostEstimate(
            flops=6 * m * width * hidden_width,
            bytes_accessed=1,
            transcendentals=m * hidden_width,
        ),
        name="experts",
    )(me, gate_weight, up_weight, down_weight, *xs, *after)


def routed_dense(hidden_in, expert_ids, gate_coef, gate_weight, up_weight, down_weight):
    n_dev = lax.axis_size("dev")
    mv = Moves(n_dev)
    weights = (gate_weight, up_weight, down_weight)
    n = mv.line
    half = n // 2
    cat = lambda *a: jnp.concatenate(a, axis=0)
    block = [pack_rows(hidden_in, expert_ids, gate_coef, n_dev)]
    for _ in range(n - 1):
        block.append(mv.ring(block[-1]))
    near = [cat(b, mv.first(b)) for b in block]
    far = [mv.second(a) for a in near]
    pairs = [a for k in range(n) for a in (near[k], far[k])]
    own = cat(*pairs[: 2 * half])
    early = expert_group([own, mv.core(own)], half, *weights, n_dev)
    rows = block[0].shape[0]
    y_near, y_far = early[0 : 2 * half : 2], early[1 : 2 * half : 2]
    order = list(range(1, n)) + [0]
    mine, crossed, back = {}, {}, []
    for k in [k for k in order if k < half]:
        mine[k] = mv.core(early[2 * half + k])
        back.append(plus(y_far[k], mine[k][2 * rows :]))
        crossed[k] = mv.second(back[-1])
    late = [cat(near[k], far[k]) for k in range(half, n - 1)] + pairs[2 * n - 2 :]
    theirs = [mv.core(a) for a in late[:-1]] + [mv.core(after(late[-1], early[-1]))]
    late = expert_group(late + theirs, n - half, *weights, n_dev, *back)
    y_near, y_far = y_near + late[0 : 2 * (n - half) : 2], y_far + late[1 : 2 * (n - half) : 2]
    acc = ()
    for k in order:
        if k >= half:
            mine[k] = mv.core(late[2 * (n - half) + k - half])
            back = plus(y_far[k], mine[k][2 * rows :])
            crossed[k] = mv.second(after(back, crossed[k - 1]) if k > half else back)
        side = mv.first(plus(y_near[k][rows:], mine[k][rows : 2 * rows], crossed[k][rows:]))
        total = plus(y_near[k][:rows], mine[k][:rows], crossed[k][:rows], side, *acc)
        if k:
            acc = (mv.ring(total),)
    return total


def per_device(
    hidden_in,
    expert_ids,
    gate_coef,
    query_lat,
    kv_cache,
    cache_len,
    gate_weight,
    up_weight,
    down_weight,
):
    half_rows = hidden_in.shape[0] // 2
    expert_count = lax.axis_size("dev")
    capacity = max(2, 2 * TOP * half_rows // expert_count)
    weights = (gate_weight, up_weight, down_weight)
    if capacity < half_rows:
        routed_out = routed_sparse(
            hidden_in, expert_ids, gate_coef, *weights, half_rows, capacity
        )
    else:
        routed_out = routed_dense(hidden_in, expert_ids, gate_coef, *weights)
    attention = attend(query_lat, kv_cache, cache_len)
    return (attention, routed_out)


def solution(mesh):
    in_specs = (
        P(("sec", "dev"), None),
        P(("sec", "dev"), None),
        P(("sec", "dev"), None),
        P(("sec", "dev"), None, None),
        P(("sec", "dev"), None, None),
        P(("sec", "dev")),
        P("dev", None, "sec"),
        P("dev", None, "sec"),
        P("dev", "sec", None),
    )
    out_specs = (P(("sec", "dev"), None, None), P(("sec", "dev"), None))
    return jax.shard_map(
        per_device, mesh=mesh, in_specs=in_specs, out_specs=out_specs, check_vma=False
    )
```

```python
import functools
import math

import jax
import jax.numpy as jnp
from jax import lax
from jax.experimental import pallas as pl
from jax.experimental.pallas import tpu as pltpu
from jax.sharding import PartitionSpec as P

LAT = 512
TOP = 8
AXES = ("sec", "dev")

score_scale = 1.0 / math.sqrt(192.0)


def attend(query_lat, kv_cache, cache_len):
    scores = (
        jnp.einsum("rhk,rlk->rhl", query_lat, kv_cache, preferred_element_type=jnp.float32)
        * score_scale
    )
    positions = jnp.arange(kv_cache.shape[1], dtype=jnp.int32)
    visible = positions[None, None, :] < cache_len[:, None, None]
    scores = jnp.where(visible, scores, jnp.float32(-1e30))
    top_score = jnp.max(scores, axis=2, keepdims=True)
    exponent = jnp.exp(scores - top_score)
    denominator = jnp.sum(exponent, axis=2, keepdims=True)
    weights = (exponent / denominator).astype(jnp.bfloat16)
    return jnp.einsum(
        "rhl,rlc->rhc", weights, kv_cache[:, :, :LAT], preferred_element_type=jnp.float32
    ).astype(jnp.bfloat16)


def routing_tables(expert_ids, gate_coef, expert_count, capacity):
    row_count, top_count = expert_ids.shape
    flat_ids = expert_ids.reshape(-1)
    position_ids = jnp.arange(flat_ids.shape[0], dtype=jnp.int32)
    matches = (flat_ids[:, None] == flat_ids[None, :]) & (
        position_ids[None, :] < position_ids[:, None]
    )
    slot_rank = jnp.sum(matches.astype(jnp.int32), axis=1)
    target = flat_ids * capacity + slot_rank
    slot_ids = jnp.arange(expert_count * capacity, dtype=jnp.int32)
    placed = (target[None, :] == slot_ids[:, None]).astype(jnp.float32)
    owner_hot = (
        (position_ids // top_count)[:, None] == jnp.arange(row_count, dtype=jnp.int32)[None, :]
    ).astype(jnp.float32)
    picker = jnp.dot(placed, owner_hot, precision=lax.Precision.HIGHEST).astype(jnp.bfloat16)
    weighted = owner_hot * gate_coef.reshape(-1)[:, None]
    mixing = jnp.dot(weighted.T, placed.T, precision=lax.Precision.HIGHEST)
    return (picker, mixing)


def expert_rows(tokens, gate_weight, up_weight, down_weight):
    shape_in = tokens.shape
    flat_rows = tokens.reshape(-1, shape_in[-1])
    gate_val = jnp.dot(flat_rows, gate_weight[0], preferred_element_type=jnp.float32)
    up_val = jnp.dot(flat_rows, up_weight[0], preferred_element_type=jnp.float32)
    hidden = (jax.nn.silu(gate_val) * up_val).astype(jnp.bfloat16)
    part_out = jnp.dot(hidden, down_weight[0], preferred_element_type=jnp.float32).astype(
        jnp.bfloat16
    )
    return part_out.reshape(shape_in)


def route_tokens(send_buf, gate_weight, up_weight, down_weight):
    section_count = lax.axis_size("sec")
    doubled = jnp.concatenate([send_buf] * section_count, axis=0)
    halves = expert_rows(
        lax.all_to_all(doubled, AXES, split_axis=0, concat_axis=0, tiled=True),
        gate_weight,
        up_weight,
        down_weight,
    )
    returned = lax.all_to_all(halves, AXES, split_axis=0, concat_axis=0, tiled=True)
    pieces = returned.reshape((section_count,) + send_buf.shape).astype(jnp.float32)
    return jnp.sum(pieces, axis=0).astype(jnp.bfloat16)


def combine(returned, mixing):
    flat_back = returned.reshape(-1, returned.shape[-1]).astype(jnp.float32)
    return jnp.dot(mixing, flat_back, precision=lax.Precision.HIGHEST).astype(jnp.bfloat16)


def routed_sparse(
    hidden_in, expert_ids, gate_coef, gate_weight, up_weight, down_weight, half_rows, capacity
):
    model_width = hidden_in.shape[1]
    expert_count = lax.axis_size("dev")
    outs = []
    for offset in (0, half_rows):
        picker, mixing = routing_tables(
            expert_ids[offset : offset + half_rows],
            gate_coef[offset : offset + half_rows],
            expert_count,
            capacity,
        )
        gathered = jnp.dot(
            picker, hidden_in[offset : offset + half_rows], preferred_element_type=jnp.float32
        ).astype(jnp.bfloat16)
        send_buf = gathered.reshape(expert_count, capacity, model_width)
        outs.append(combine(route_tokens(send_buf, gate_weight, up_weight, down_weight), mixing))
    return jnp.concatenate(outs, axis=0)


def permutation(n_dev, move):
    pairs = []
    for y in range(2):
        for d in range(n_dev):
            there = move(y, d // 4, (d // 2) % 2, d % 2)
            if there is not None:
                ty, tz, tx, tc = there
                pairs.append((y * n_dev + d, ty * n_dev + tz * 4 + tx * 2 + tc))
    return lambda a: lax.ppermute(a, AXES, pairs)


class Moves:
    def __init__(self, n_dev):
        line = n_dev // 4
        self.line = line
        self.core = permutation(n_dev, lambda y, z, x, c: (y, z, x, 1 - c))
        self.first = permutation(
            n_dev, lambda y, z, x, c: (1 - y, z, x, c) if c else (y, z, 1 - x, c)
        )
        self.second = permutation(
            n_dev, lambda y, z, x, c: (y, z, 1 - x, c) if c else (1 - y, z, x, c)
        )
        stops = list(range(0, line, 2)) + list(range(1, line, 2))[::-1]
        following = {z: stops[(i + 1) % line] for i, z in enumerate(stops)}
        self.ring = permutation(n_dev, lambda y, z, x, c: (y, following[z], x, c))


def plus(*terms):
    total = terms[0].astype(jnp.float32)
    for t in terms[1:]:
        total = total + t.astype(jnp.float32)
    return total.astype(jnp.bfloat16)


def after(a, other):
    return a + other[:1, :1] * 0


ANYWHERE = pl.BlockSpec(memory_space=pl.ANY)
FAR = pl.BlockSpec(memory_space=pltpu.HBM)
HELD = pl.BlockSpec(memory_space=pltpu.VMEM)
SCALARS = pl.BlockSpec(memory_space=pltpu.SMEM)


def pack_kernel(n_experts, ids, coefs, x, out):
    rows, width = x.shape
    hot = lax.broadcasted_iota(jnp.int32, (n_experts, rows), 0)
    dense = jnp.zeros((n_experts, rows), jnp.float32)
    for k in range(ids.shape[0]):
        dense += jnp.where(hot == ids[k : k + 1, :], coefs[k : k + 1, :], 0.0)
    high = dense.astype(jnp.bfloat16)
    low = (dense - high.astype(jnp.float32)).astype(jnp.bfloat16)
    rest = jnp.zeros((out.shape[1] - width - 2 * n_experts, rows), jnp.bfloat16)
    parts = jnp.concatenate([high, low, rest], axis=0)
    same = lax.broadcasted_iota(jnp.int32, (rows, rows), 0) == lax.broadcasted_iota(
        jnp.int32, (rows, rows), 1
    )
    turned = lax.dot_general(
        same.astype(jnp.bfloat16),
        parts,
        (((1,), (1,)), ((), ())),
        preferred_element_type=jnp.float32,
    )
    out[:, :width] = x[...]
    out[:, width:] = turned.astype(jnp.bfloat16)


def pack_rows(hidden_in, expert_ids, gate_coef, n_experts):
    rows, width = hidden_in.shape
    tail = 2 * n_experts + -2 * n_experts % 128
    return pl.pallas_call(
        functools.partial(pack_kernel, n_experts),
        in_specs=[HELD] * 3,
        out_specs=HELD,
        out_shape=jax.ShapeDtypeStruct((rows, width + tail), jnp.bfloat16),
        name="pack",
    )(expert_ids.T, gate_coef.T, hidden_in)


def hold_kernel(weight, *refs):
    refs[-1][...] = jnp.zeros(refs[-1].shape, refs[-1].dtype)


def hold(weight, *after):
    return pl.pallas_call(
        hold_kernel,
        in_specs=[HELD] + [ANYWHERE] * len(after),
        out_specs=HELD,
        out_shape=jax.ShapeDtypeStruct((8, 128), jnp.float32),
        compiler_params=pltpu.CompilerParams(vmem_limit_bytes=1 * 2**20),
        cost_estimate=pl.CostEstimate(
            flops=0, bytes_accessed=2 * math.prod(weight.shape), transcendentals=0
        ),
        name="hold",
    )(weight, *after)


def expert_kernel(sizes, sizes_out, n_experts, steps, me, w_gate, w_up, w_down, *refs):
    xs = refs[: len(sizes)]
    outs = refs[-4 - len(sizes_out) : -4]
    acc_gate, acc_up, hidden, coef = refs[-4:]
    width = w_gate.shape[1]
    chunk = width // steps
    part = [pl.ds(k * chunk, chunk) for k in range(steps)]
    tail = jnp.concatenate([x[:, width:] for x in xs], axis=0).astype(jnp.float32)
    lane = lax.broadcasted_iota(jnp.int32, tail.shape, 1)
    mine = (lane == me[0]) | (lane == me[0] + n_experts)
    picked = jnp.sum(jnp.where(mine, tail, 0.0), axis=1, keepdims=True)
    coef[...] = jnp.broadcast_to(picked, coef.shape)
    for k in range(steps):
        xk = jnp.concatenate([x[:, part[k]] for x in xs], axis=0)
        g = jnp.dot(xk, w_gate[0, part[k], :], preferred_element_type=jnp.float32)
        u = jnp.dot(xk, w_up[0, part[k], :], preferred_element_type=jnp.float32)
        if k == 0:
            acc_gate[...] = g
            acc_up[...] = u
        else:
            acc_gate[...] += g
            acc_up[...] += u
    g = acc_gate[...]
    hidden[...] = (g / (1.0 + jnp.exp(-g)) * acc_up[...]).astype(jnp.bfloat16)
    for k in range(steps):
        yk = jnp.dot(hidden[...], w_down[0, :, part[k]], preferred_element_type=jnp.float32)
        yk = (yk * coef[:, :1]).astype(jnp.bfloat16)
        row = 0
        for out in outs:
            out[:, part[k]] = yk[row : row + out.shape[0]]
            row += out.shape[0]


def expert_group(xs, slots, gate_weight, up_weight, down_weight, n_experts, *after):
    sizes = [x.shape[0] for x in xs]
    m = sum(sizes)
    _, width, hidden_width = gate_weight.shape
    chunk = max(c for c in range(128, 1025, 128) if width % c == 0)
    steps = width // chunk
    quarter = m // slots // 4
    outs = [quarter] * (2 * slots) + [2 * quarter] * slots
    me = lax.axis_index("dev").astype(jnp.int32).reshape(1)
    return pl.pallas_call(
        functools.partial(expert_kernel, sizes, outs, n_experts, steps),
        in_specs=[SCALARS] + [HELD] * 3 + [HELD] * len(xs) + [ANYWHERE] * len(after),
        out_specs=[HELD] * len(outs),
        scratch_shapes=[
            pltpu.VMEM((m, hidden_width), jnp.float32),
            pltpu.VMEM((m, hidden_width), jnp.float32),
            pltpu.VMEM((m, hidden_width), jnp.bfloat16),
            pltpu.VMEM((m, 128), jnp.float32),
        ],
        out_shape=[jax.ShapeDtypeStruct((r, width), jnp.bfloat16) for r in outs],
        compiler_params=pltpu.CompilerParams(vmem_limit_bytes=8 * 2**20),
        cost_estimate=pl.CostEstimate(
            flops=6 * m * width * hidden_width,
            bytes_accessed=1,
            transcendentals=m * hidden_width,
        ),
        name="experts",
    )(me, gate_weight, up_weight, down_weight, *xs, *after)


def routed_dense(hidden_in, expert_ids, gate_coef, gate_weight, up_weight, down_weight):
    n_dev = lax.axis_size("dev")
    mv = Moves(n_dev)
    weights = (gate_weight, up_weight, down_weight)
    n = mv.line
    half = n // 2
    cat = lambda *a: jnp.concatenate(a, axis=0)
    block = [pack_rows(hidden_in, expert_ids, gate_coef, n_dev)]
    for _ in range(n - 1):
        block.append(mv.ring(block[-1]))
    near = [cat(b, mv.first(b)) for b in block]
    far = [mv.second(a) for a in near]
    pairs = [a for k in range(n) for a in (near[k], far[k])]
    own = cat(*pairs[: 2 * half])
    held = [hold(w, a) for w, a in zip(weights, (block[1], block[2], near[2]))]
    early = expert_group([own, mv.core(own)], half, *weights, n_dev, *held)
    rows = block[0].shape[0]
    y_near, y_far = early[0 : 2 * half : 2], early[1 : 2 * half : 2]
    order = list(range(1, n)) + [0]
    mine, crossed, back = {}, {}, []
    for k in [k for k in order if k < half]:
        mine[k] = mv.core(early[2 * half + k])
        back.append(plus(y_far[k], mine[k][2 * rows :]))
        crossed[k] = mv.second(back[-1])
    late = [cat(near[k], far[k]) for k in range(half, n - 1)] + pairs[2 * n - 2 :]
    theirs = [mv.core(a) for a in late[:-1]] + [mv.core(after(late[-1], early[-1]))]
    late = expert_group(late + theirs, n - half, *weights, n_dev, *back)
    y_near, y_far = y_near + late[0 : 2 * (n - half) : 2], y_far + late[1 : 2 * (n - half) : 2]
    acc = ()
    for k in order:
        if k >= half:
            mine[k] = mv.core(late[2 * (n - half) + k - half])
            back = plus(y_far[k], mine[k][2 * rows :])
            crossed[k] = mv.second(after(back, crossed[k - 1]) if k > half else back)
        side = mv.first(plus(y_near[k][rows:], mine[k][rows : 2 * rows], crossed[k][rows:]))
        total = plus(y_near[k][:rows], mine[k][:rows], crossed[k][:rows], side, *acc)
        if k:
            acc = (mv.ring(total),)
    return total


def per_device(
    hidden_in,
    expert_ids,
    gate_coef,
    query_lat,
    kv_cache,
    cache_len,
    gate_weight,
    up_weight,
    down_weight,
):
    half_rows = hidden_in.shape[0] // 2
    expert_count = lax.axis_size("dev")
    capacity = max(2, 2 * TOP * half_rows // expert_count)
    weights = (gate_weight, up_weight, down_weight)
    if capacity < half_rows:
        routed_out = routed_sparse(
            hidden_in, expert_ids, gate_coef, *weights, half_rows, capacity
        )
    else:
        routed_out = routed_dense(hidden_in, expert_ids, gate_coef, *weights)
    attention = attend(query_lat, kv_cache, cache_len)
    return (attention, routed_out)


def solution(mesh):
    in_specs = (
        P(("sec", "dev"), None),
        P(("sec", "dev"), None),
        P(("sec", "dev"), None),
        P(("sec", "dev"), None, None),
        P(("sec", "dev"), None, None),
        P(("sec", "dev")),
        P("dev", None, "sec"),
        P("dev", None, "sec"),
        P("dev", "sec", None),
    )
    out_specs = (P(("sec", "dev"), None, None), P(("sec", "dev"), None))
    return jax.shard_map(
        per_device, mesh=mesh, in_specs=in_specs, out_specs=out_specs, check_vma=False
    )
```

```python
import functools
import math

import jax
import jax.numpy as jnp
from jax import lax
from jax.experimental import pallas as pl
from jax.experimental.pallas import tpu as pltpu
from jax.sharding import PartitionSpec as P

LAT = 512
TOP = 8
AXES = ("sec", "dev")

score_scale = 1.0 / math.sqrt(192.0)


def attend(query_lat, kv_cache, cache_len):
    scores = (
        jnp.einsum("rhk,rlk->rhl", query_lat, kv_cache, preferred_element_type=jnp.float32)
        * score_scale
    )
    positions = jnp.arange(kv_cache.shape[1], dtype=jnp.int32)
    visible = positions[None, None, :] < cache_len[:, None, None]
    scores = jnp.where(visible, scores, jnp.float32(-1e30))
    top_score = jnp.max(scores, axis=2, keepdims=True)
    exponent = jnp.exp(scores - top_score)
    denominator = jnp.sum(exponent, axis=2, keepdims=True)
    weights = (exponent / denominator).astype(jnp.bfloat16)
    return jnp.einsum(
        "rhl,rlc->rhc", weights, kv_cache[:, :, :LAT], preferred_element_type=jnp.float32
    ).astype(jnp.bfloat16)


def routing_tables(expert_ids, gate_coef, expert_count, capacity):
    row_count, top_count = expert_ids.shape
    flat_ids = expert_ids.reshape(-1)
    position_ids = jnp.arange(flat_ids.shape[0], dtype=jnp.int32)
    matches = (flat_ids[:, None] == flat_ids[None, :]) & (
        position_ids[None, :] < position_ids[:, None]
    )
    slot_rank = jnp.sum(matches.astype(jnp.int32), axis=1)
    target = flat_ids * capacity + slot_rank
    slot_ids = jnp.arange(expert_count * capacity, dtype=jnp.int32)
    placed = (target[None, :] == slot_ids[:, None]).astype(jnp.float32)
    owner_hot = (
        (position_ids // top_count)[:, None] == jnp.arange(row_count, dtype=jnp.int32)[None, :]
    ).astype(jnp.float32)
    picker = jnp.dot(placed, owner_hot, precision=lax.Precision.HIGHEST).astype(jnp.bfloat16)
    weighted = owner_hot * gate_coef.reshape(-1)[:, None]
    mixing = jnp.dot(weighted.T, placed.T, precision=lax.Precision.HIGHEST)
    return (picker, mixing)


def expert_rows(tokens, gate_weight, up_weight, down_weight):
    shape_in = tokens.shape
    flat_rows = tokens.reshape(-1, shape_in[-1])
    gate_val = jnp.dot(flat_rows, gate_weight[0], preferred_element_type=jnp.float32)
    up_val = jnp.dot(flat_rows, up_weight[0], preferred_element_type=jnp.float32)
    hidden = (jax.nn.silu(gate_val) * up_val).astype(jnp.bfloat16)
    part_out = jnp.dot(hidden, down_weight[0], preferred_element_type=jnp.float32).astype(
        jnp.bfloat16
    )
    return part_out.reshape(shape_in)


def route_tokens(send_buf, gate_weight, up_weight, down_weight):
    section_count = lax.axis_size("sec")
    doubled = jnp.concatenate([send_buf] * section_count, axis=0)
    halves = expert_rows(
        lax.all_to_all(doubled, AXES, split_axis=0, concat_axis=0, tiled=True),
        gate_weight,
        up_weight,
        down_weight,
    )
    returned = lax.all_to_all(halves, AXES, split_axis=0, concat_axis=0, tiled=True)
    pieces = returned.reshape((section_count,) + send_buf.shape).astype(jnp.float32)
    return jnp.sum(pieces, axis=0).astype(jnp.bfloat16)


def combine(returned, mixing):
    flat_back = returned.reshape(-1, returned.shape[-1]).astype(jnp.float32)
    return jnp.dot(mixing, flat_back, precision=lax.Precision.HIGHEST).astype(jnp.bfloat16)


def routed_sparse(
    hidden_in, expert_ids, gate_coef, gate_weight, up_weight, down_weight, half_rows, capacity
):
    model_width = hidden_in.shape[1]
    expert_count = lax.axis_size("dev")
    outs = []
    for offset in (0, half_rows):
        picker, mixing = routing_tables(
            expert_ids[offset : offset + half_rows],
            gate_coef[offset : offset + half_rows],
            expert_count,
            capacity,
        )
        gathered = jnp.dot(
            picker, hidden_in[offset : offset + half_rows], preferred_element_type=jnp.float32
        ).astype(jnp.bfloat16)
        send_buf = gathered.reshape(expert_count, capacity, model_width)
        outs.append(combine(route_tokens(send_buf, gate_weight, up_weight, down_weight), mixing))
    return jnp.concatenate(outs, axis=0)


def permutation(n_dev, move):
    pairs = []
    for y in range(2):
        for d in range(n_dev):
            there = move(y, d // 4, (d // 2) % 2, d % 2)
            if there is not None:
                ty, tz, tx, tc = there
                pairs.append((y * n_dev + d, ty * n_dev + tz * 4 + tx * 2 + tc))
    return lambda a: lax.ppermute(a, AXES, pairs)


class Moves:
    def __init__(self, n_dev):
        line = n_dev // 4
        self.line = line
        self.core = permutation(n_dev, lambda y, z, x, c: (y, z, x, 1 - c))
        self.first = permutation(
            n_dev, lambda y, z, x, c: (1 - y, z, x, c) if c else (y, z, 1 - x, c)
        )
        self.second = permutation(
            n_dev, lambda y, z, x, c: (y, z, 1 - x, c) if c else (1 - y, z, x, c)
        )
        stops = list(range(0, line, 2)) + list(range(1, line, 2))[::-1]
        following = {z: stops[(i + 1) % line] for i, z in enumerate(stops)}
        self.ring = permutation(n_dev, lambda y, z, x, c: (y, following[z], x, c))


def plus(*terms):
    total = terms[0].astype(jnp.float32)
    for t in terms[1:]:
        total = total + t.astype(jnp.float32)
    return total.astype(jnp.bfloat16)


def after(a, other):
    return a + other[:1, :1] * 0


ANYWHERE = pl.BlockSpec(memory_space=pl.ANY)
FAR = pl.BlockSpec(memory_space=pltpu.HBM)
HELD = pl.BlockSpec(memory_space=pltpu.VMEM)
SCALARS = pl.BlockSpec(memory_space=pltpu.SMEM)


def pack_kernel(n_experts, ids, coefs, x, out):
    rows, width = x.shape
    hot = lax.broadcasted_iota(jnp.int32, (n_experts, rows), 0)
    dense = jnp.zeros((n_experts, rows), jnp.float32)
    for k in range(ids.shape[0]):
        dense += jnp.where(hot == ids[k : k + 1, :], coefs[k : k + 1, :], 0.0)
    high = dense.astype(jnp.bfloat16)
    low = (dense - high.astype(jnp.float32)).astype(jnp.bfloat16)
    rest = jnp.zeros((out.shape[1] - width - 2 * n_experts, rows), jnp.bfloat16)
    parts = jnp.concatenate([high, low, rest], axis=0)
    same = lax.broadcasted_iota(jnp.int32, (rows, rows), 0) == lax.broadcasted_iota(
        jnp.int32, (rows, rows), 1
    )
    turned = lax.dot_general(
        same.astype(jnp.bfloat16),
        parts,
        (((1,), (1,)), ((), ())),
        preferred_element_type=jnp.float32,
    )
    out[:, :width] = x[...]
    out[:, width:] = turned.astype(jnp.bfloat16)


def pack_rows(hidden_in, expert_ids, gate_coef, n_experts):
    rows, width = hidden_in.shape
    tail = 2 * n_experts + -2 * n_experts % 128
    return pl.pallas_call(
        functools.partial(pack_kernel, n_experts),
        in_specs=[HELD] * 3,
        out_specs=HELD,
        out_shape=jax.ShapeDtypeStruct((rows, width + tail), jnp.bfloat16),
        name="pack",
    )(expert_ids.T, gate_coef.T, hidden_in)


def attend_kernel(lengths, q, kv, *refs):
    out = refs[-1]
    rows, heads, _ = q.shape
    slots = kv.shape[2]
    base = pl.program_id(0) * rows
    position = lax.broadcasted_iota(jnp.int32, (heads, slots), 1)
    scores = []
    for r in range(rows):
        s = jnp.dot(q[r], kv[r], preferred_element_type=jnp.float32) * score_scale
        scores.append(jnp.where(position < lengths[base + r], s, -1e30))
    scores = jnp.concatenate(scores, axis=0)
    exponent = jnp.exp(scores - jnp.max(scores, axis=1, keepdims=True))
    weights = exponent / jnp.sum(exponent, axis=1, keepdims=True)
    weights = weights.astype(jnp.bfloat16)
    for r in range(rows):
        out[r] = lax.dot_general(
            weights[r * heads : (r + 1) * heads],
            kv[r, : out.shape[2]],
            (((1,), (1,)), ((), ())),
            preferred_element_type=jnp.float32,
        ).astype(jnp.bfloat16)


def attend_rows(query_lat, kv_cache, cache_len, *after):
    rows, heads, width = query_lat.shape
    slots = kv_cache.shape[1]
    step = max(s for s in (8, 1) if rows % s == 0)
    return pl.pallas_call(
        attend_kernel,
        grid=(rows // step,),
        in_specs=[
            SCALARS,
            pl.BlockSpec((step, heads, width), lambda i: (i, 0, 0)),
            pl.BlockSpec((step, width, slots), lambda i: (i, 0, 0)),
        ]
        + [ANYWHERE] * len(after),
        out_specs=pl.BlockSpec((step, heads, LAT), lambda i: (i, 0, 0)),
        out_shape=jax.ShapeDtypeStruct((rows, heads, LAT), jnp.bfloat16),
        compiler_params=pltpu.CompilerParams(vmem_limit_bytes=40 * 2**20),
        cost_estimate=pl.CostEstimate(
            flops=20 * rows * heads * slots * (width + LAT), bytes_accessed=1, transcendentals=0
        ),
        name="attend",
    )(cache_len, query_lat, jnp.swapaxes(kv_cache, 1, 2), *after)


def hold_kernel(weight, *refs):
    refs[-1][...] = jnp.zeros(refs[-1].shape, refs[-1].dtype)


def hold(weight, *after):
    return pl.pallas_call(
        hold_kernel,
        in_specs=[HELD] + [ANYWHERE] * len(after),
        out_specs=HELD,
        out_shape=jax.ShapeDtypeStruct((8, 128), jnp.float32),
        compiler_params=pltpu.CompilerParams(vmem_limit_bytes=1 * 2**20),
        cost_estimate=pl.CostEstimate(
            flops=0, bytes_accessed=2 * math.prod(weight.shape), transcendentals=0
        ),
        name="hold",
    )(weight, *after)


def expert_kernel(sizes, sizes_out, n_experts, steps, me, w_gate, w_up, w_down, *refs):
    xs = refs[: len(sizes)]
    outs = refs[-4 - len(sizes_out) : -4]
    acc_gate, acc_up, hidden, coef = refs[-4:]
    width = w_gate.shape[1]
    chunk = width // steps
    part = [pl.ds(k * chunk, chunk) for k in range(steps)]
    tail = jnp.concatenate([x[:, width:] for x in xs], axis=0).astype(jnp.float32)
    lane = lax.broadcasted_iota(jnp.int32, tail.shape, 1)
    mine = (lane == me[0]) | (lane == me[0] + n_experts)
    picked = jnp.sum(jnp.where(mine, tail, 0.0), axis=1, keepdims=True)
    coef[...] = jnp.broadcast_to(picked, coef.shape)
    for k in range(steps):
        xk = jnp.concatenate([x[:, part[k]] for x in xs], axis=0)
        g = jnp.dot(xk, w_gate[0, part[k], :], preferred_element_type=jnp.float32)
        u = jnp.dot(xk, w_up[0, part[k], :], preferred_element_type=jnp.float32)
        if k == 0:
            acc_gate[...] = g
            acc_up[...] = u
        else:
            acc_gate[...] += g
            acc_up[...] += u
    g = acc_gate[...]
    hidden[...] = (g / (1.0 + jnp.exp(-g)) * acc_up[...]).astype(jnp.bfloat16)
    for k in range(steps):
        yk = jnp.dot(hidden[...], w_down[0, :, part[k]], preferred_element_type=jnp.float32)
        yk = (yk * coef[:, :1]).astype(jnp.bfloat16)
        row = 0
        for out in outs:
            out[:, part[k]] = yk[row : row + out.shape[0]]
            row += out.shape[0]


def expert_group(xs, slots, gate_weight, up_weight, down_weight, n_experts, *after):
    sizes = [x.shape[0] for x in xs]
    m = sum(sizes)
    _, width, hidden_width = gate_weight.shape
    chunk = max(c for c in range(128, 1025, 128) if width % c == 0)
    steps = width // chunk
    quarter = m // slots // 4
    outs = [quarter] * (2 * slots) + [2 * quarter] * slots
    me = lax.axis_index("dev").astype(jnp.int32).reshape(1)
    return pl.pallas_call(
        functools.partial(expert_kernel, sizes, outs, n_experts, steps),
        in_specs=[SCALARS] + [HELD] * 3 + [HELD] * len(xs) + [ANYWHERE] * len(after),
        out_specs=[HELD] * len(outs),
        scratch_shapes=[
            pltpu.VMEM((m, hidden_width), jnp.float32),
            pltpu.VMEM((m, hidden_width), jnp.float32),
            pltpu.VMEM((m, hidden_width), jnp.bfloat16),
            pltpu.VMEM((m, 128), jnp.float32),
        ],
        out_shape=[jax.ShapeDtypeStruct((r, width), jnp.bfloat16) for r in outs],
        compiler_params=pltpu.CompilerParams(vmem_limit_bytes=8 * 2**20),
        cost_estimate=pl.CostEstimate(
            flops=6 * m * width * hidden_width,
            bytes_accessed=1,
            transcendentals=m * hidden_width,
        ),
        name="experts",
    )(me, gate_weight, up_weight, down_weight, *xs, *after)


def routed_dense(hidden_in, expert_ids, gate_coef, gate_weight, up_weight, down_weight):
    n_dev = lax.axis_size("dev")
    mv = Moves(n_dev)
    weights = (gate_weight, up_weight, down_weight)
    n = mv.line
    half = n // 2
    cat = lambda *a: jnp.concatenate(a, axis=0)
    block = [pack_rows(hidden_in, expert_ids, gate_coef, n_dev)]
    for _ in range(n - 1):
        block.append(mv.ring(block[-1]))
    near = [cat(b, mv.first(b)) for b in block]
    far = [mv.second(a) for a in near]
    pairs = [a for k in range(n) for a in (near[k], far[k])]
    own = cat(*pairs[: 2 * half])
    held = [hold(w, a) for w, a in zip(weights, (block[1], block[2], near[2]))]
    early = expert_group([own, mv.core(own)], half, *weights, n_dev, *held)
    rows = block[0].shape[0]
    y_near, y_far = early[0 : 2 * half : 2], early[1 : 2 * half : 2]
    order = list(range(1, n)) + [0]
    mine, crossed, back = {}, {}, []
    for k in [k for k in order if k < half]:
        mine[k] = mv.core(early[2 * half + k])
        back.append(plus(y_far[k], mine[k][2 * rows :]))
        crossed[k] = mv.second(back[-1])
    late = [cat(near[k], far[k]) for k in range(half, n - 1)] + pairs[2 * n - 2 :]
    theirs = [mv.core(a) for a in late[:-1]] + [mv.core(after(late[-1], early[-1]))]
    late = expert_group(late + theirs, n - half, *weights, n_dev, *back)
    y_near, y_far = y_near + late[0 : 2 * (n - half) : 2], y_far + late[1 : 2 * (n - half) : 2]
    acc = ()
    for k in order:
        if k >= half:
            mine[k] = mv.core(late[2 * (n - half) + k - half])
            back = plus(y_far[k], mine[k][2 * rows :])
            crossed[k] = mv.second(after(back, crossed[k - 1]) if k > half else back)
        side = mv.first(plus(y_near[k][rows:], mine[k][rows : 2 * rows], crossed[k][rows:]))
        total = plus(y_near[k][:rows], mine[k][:rows], crossed[k][:rows], side, *acc)
        if k:
            acc = (mv.ring(total),)
    return total


def per_device(
    hidden_in,
    expert_ids,
    gate_coef,
    query_lat,
    kv_cache,
    cache_len,
    gate_weight,
    up_weight,
    down_weight,
):
    half_rows = hidden_in.shape[0] // 2
    expert_count = lax.axis_size("dev")
    capacity = max(2, 2 * TOP * half_rows // expert_count)
    weights = (gate_weight, up_weight, down_weight)
    if capacity < half_rows:
        routed_out = routed_sparse(
            hidden_in, expert_ids, gate_coef, *weights, half_rows, capacity
        )
        attention = attend(query_lat, kv_cache, cache_len)
    else:
        routed_out = routed_dense(hidden_in, expert_ids, gate_coef, *weights)
        attention = attend_rows(query_lat, kv_cache, cache_len)
    return (attention, routed_out)


def solution(mesh):
    in_specs = (
        P(("sec", "dev"), None),
        P(("sec", "dev"), None),
        P(("sec", "dev"), None),
        P(("sec", "dev"), None, None),
        P(("sec", "dev"), None, None),
        P(("sec", "dev")),
        P("dev", None, "sec"),
        P("dev", None, "sec"),
        P("dev", "sec", None),
    )
    out_specs = (P(("sec", "dev"), None, None), P(("sec", "dev"), None))
    return jax.shard_map(
        per_device, mesh=mesh, in_specs=in_specs, out_specs=out_specs, check_vma=False
    )
```

```python
import functools
import math

import jax
import jax.numpy as jnp
from jax import lax
from jax.experimental import pallas as pl
from jax.experimental.pallas import tpu as pltpu
from jax.sharding import PartitionSpec as P

LAT = 512
TOP = 8
AXES = ("sec", "dev")

score_scale = 1.0 / math.sqrt(192.0)


def attend(query_lat, kv_cache, cache_len):
    scores = (
        jnp.einsum("rhk,rlk->rhl", query_lat, kv_cache, preferred_element_type=jnp.float32)
        * score_scale
    )
    positions = jnp.arange(kv_cache.shape[1], dtype=jnp.int32)
    visible = positions[None, None, :] < cache_len[:, None, None]
    scores = jnp.where(visible, scores, jnp.float32(-1e30))
    top_score = jnp.max(scores, axis=2, keepdims=True)
    exponent = jnp.exp(scores - top_score)
    denominator = jnp.sum(exponent, axis=2, keepdims=True)
    weights = (exponent / denominator).astype(jnp.bfloat16)
    return jnp.einsum(
        "rhl,rlc->rhc", weights, kv_cache[:, :, :LAT], preferred_element_type=jnp.float32
    ).astype(jnp.bfloat16)


def routing_tables(expert_ids, gate_coef, expert_count, capacity):
    row_count, top_count = expert_ids.shape
    flat_ids = expert_ids.reshape(-1)
    position_ids = jnp.arange(flat_ids.shape[0], dtype=jnp.int32)
    matches = (flat_ids[:, None] == flat_ids[None, :]) & (
        position_ids[None, :] < position_ids[:, None]
    )
    slot_rank = jnp.sum(matches.astype(jnp.int32), axis=1)
    target = flat_ids * capacity + slot_rank
    slot_ids = jnp.arange(expert_count * capacity, dtype=jnp.int32)
    placed = (target[None, :] == slot_ids[:, None]).astype(jnp.float32)
    owner_hot = (
        (position_ids // top_count)[:, None] == jnp.arange(row_count, dtype=jnp.int32)[None, :]
    ).astype(jnp.float32)
    picker = jnp.dot(placed, owner_hot, precision=lax.Precision.HIGHEST).astype(jnp.bfloat16)
    weighted = owner_hot * gate_coef.reshape(-1)[:, None]
    mixing = jnp.dot(weighted.T, placed.T, precision=lax.Precision.HIGHEST)
    return (picker, mixing)


def expert_rows(tokens, gate_weight, up_weight, down_weight):
    shape_in = tokens.shape
    flat_rows = tokens.reshape(-1, shape_in[-1])
    gate_val = jnp.dot(flat_rows, gate_weight[0], preferred_element_type=jnp.float32)
    up_val = jnp.dot(flat_rows, up_weight[0], preferred_element_type=jnp.float32)
    hidden = (jax.nn.silu(gate_val) * up_val).astype(jnp.bfloat16)
    part_out = jnp.dot(hidden, down_weight[0], preferred_element_type=jnp.float32).astype(
        jnp.bfloat16
    )
    return part_out.reshape(shape_in)


def route_tokens(send_buf, gate_weight, up_weight, down_weight):
    section_count = lax.axis_size("sec")
    doubled = jnp.concatenate([send_buf] * section_count, axis=0)
    halves = expert_rows(
        lax.all_to_all(doubled, AXES, split_axis=0, concat_axis=0, tiled=True),
        gate_weight,
        up_weight,
        down_weight,
    )
    returned = lax.all_to_all(halves, AXES, split_axis=0, concat_axis=0, tiled=True)
    pieces = returned.reshape((section_count,) + send_buf.shape).astype(jnp.float32)
    return jnp.sum(pieces, axis=0).astype(jnp.bfloat16)


def combine(returned, mixing):
    flat_back = returned.reshape(-1, returned.shape[-1]).astype(jnp.float32)
    return jnp.dot(mixing, flat_back, precision=lax.Precision.HIGHEST).astype(jnp.bfloat16)


def routed_sparse(
    hidden_in, expert_ids, gate_coef, gate_weight, up_weight, down_weight, half_rows, capacity
):
    model_width = hidden_in.shape[1]
    expert_count = lax.axis_size("dev")
    outs = []
    for offset in (0, half_rows):
        picker, mixing = routing_tables(
            expert_ids[offset : offset + half_rows],
            gate_coef[offset : offset + half_rows],
            expert_count,
            capacity,
        )
        gathered = jnp.dot(
            picker, hidden_in[offset : offset + half_rows], preferred_element_type=jnp.float32
        ).astype(jnp.bfloat16)
        send_buf = gathered.reshape(expert_count, capacity, model_width)
        outs.append(combine(route_tokens(send_buf, gate_weight, up_weight, down_weight), mixing))
    return jnp.concatenate(outs, axis=0)


def permutation(n_dev, move):
    pairs = []
    for y in range(2):
        for d in range(n_dev):
            there = move(y, d // 4, (d // 2) % 2, d % 2)
            if there is not None:
                ty, tz, tx, tc = there
                pairs.append((y * n_dev + d, ty * n_dev + tz * 4 + tx * 2 + tc))
    return lambda a: lax.ppermute(a, AXES, pairs)


class Moves:
    def __init__(self, n_dev):
        line = n_dev // 4
        self.line = line
        self.core = permutation(n_dev, lambda y, z, x, c: (y, z, x, 1 - c))
        self.first = permutation(
            n_dev, lambda y, z, x, c: (1 - y, z, x, c) if c else (y, z, 1 - x, c)
        )
        self.second = permutation(
            n_dev, lambda y, z, x, c: (y, z, 1 - x, c) if c else (1 - y, z, x, c)
        )
        stops = list(range(0, line, 2)) + list(range(1, line, 2))[::-1]
        following = {z: stops[(i + 1) % line] for i, z in enumerate(stops)}
        before = {t: z for z, t in following.items()}
        self.ring = permutation(n_dev, lambda y, z, x, c: (y, following[z], x, c))
        self.ring_back = permutation(n_dev, lambda y, z, x, c: (y, before[z], x, c))


def plus(*terms):
    total = terms[0].astype(jnp.float32)
    for t in terms[1:]:
        total = total + t.astype(jnp.float32)
    return total.astype(jnp.bfloat16)


def after(a, other):
    return a + other[:1, :1] * 0


ANYWHERE = pl.BlockSpec(memory_space=pl.ANY)
FAR = pl.BlockSpec(memory_space=pltpu.HBM)
HELD = pl.BlockSpec(memory_space=pltpu.VMEM)
SCALARS = pl.BlockSpec(memory_space=pltpu.SMEM)


def pack_kernel(n_experts, ids, coefs, x, out):
    rows, width = x.shape
    hot = lax.broadcasted_iota(jnp.int32, (n_experts, rows), 0)
    dense = jnp.zeros((n_experts, rows), jnp.float32)
    for k in range(ids.shape[0]):
        dense += jnp.where(hot == ids[k : k + 1, :], coefs[k : k + 1, :], 0.0)
    high = dense.astype(jnp.bfloat16)
    low = (dense - high.astype(jnp.float32)).astype(jnp.bfloat16)
    rest = jnp.zeros((out.shape[1] - width - 2 * n_experts, rows), jnp.bfloat16)
    parts = jnp.concatenate([high, low, rest], axis=0)
    same = lax.broadcasted_iota(jnp.int32, (rows, rows), 0) == lax.broadcasted_iota(
        jnp.int32, (rows, rows), 1
    )
    turned = lax.dot_general(
        same.astype(jnp.bfloat16),
        parts,
        (((1,), (1,)), ((), ())),
        preferred_element_type=jnp.float32,
    )
    out[:, :width] = x[...]
    out[:, width:] = turned.astype(jnp.bfloat16)


def pack_rows(hidden_in, expert_ids, gate_coef, n_experts):
    rows, width = hidden_in.shape
    tail = 2 * n_experts + -2 * n_experts % 128
    return pl.pallas_call(
        functools.partial(pack_kernel, n_experts),
        in_specs=[HELD] * 3,
        out_specs=HELD,
        out_shape=jax.ShapeDtypeStruct((rows, width + tail), jnp.bfloat16),
        name="pack",
    )(expert_ids.T, gate_coef.T, hidden_in)


def attend_kernel(lengths, q, kv, *refs):
    out = refs[-1]
    rows, heads, _ = q.shape
    slots = kv.shape[2]
    base = pl.program_id(0) * rows
    position = lax.broadcasted_iota(jnp.int32, (heads, slots), 1)
    scores = []
    for r in range(rows):
        s = jnp.dot(q[r], kv[r], preferred_element_type=jnp.float32) * score_scale
        scores.append(jnp.where(position < lengths[base + r], s, -1e30))
    scores = jnp.concatenate(scores, axis=0)
    exponent = jnp.exp(scores - jnp.max(scores, axis=1, keepdims=True))
    weights = exponent / jnp.sum(exponent, axis=1, keepdims=True)
    weights = weights.astype(jnp.bfloat16)
    for r in range(rows):
        out[r] = lax.dot_general(
            weights[r * heads : (r + 1) * heads],
            kv[r, : out.shape[2]],
            (((1,), (1,)), ((), ())),
            preferred_element_type=jnp.float32,
        ).astype(jnp.bfloat16)


def attend_rows(query_lat, kv_cache, cache_len, *after):
    rows, heads, width = query_lat.shape
    slots = kv_cache.shape[1]
    step = max(s for s in (8, 1) if rows % s == 0)
    return pl.pallas_call(
        attend_kernel,
        grid=(rows // step,),
        in_specs=[
            SCALARS,
            pl.BlockSpec((step, heads, width), lambda i: (i, 0, 0)),
            pl.BlockSpec((step, width, slots), lambda i: (i, 0, 0)),
        ]
        + [ANYWHERE] * len(after),
        out_specs=pl.BlockSpec((step, heads, LAT), lambda i: (i, 0, 0)),
        out_shape=jax.ShapeDtypeStruct((rows, heads, LAT), jnp.bfloat16),
        compiler_params=pltpu.CompilerParams(vmem_limit_bytes=40 * 2**20),
        cost_estimate=pl.CostEstimate(
            flops=20 * rows * heads * slots * (width + LAT), bytes_accessed=1, transcendentals=0
        ),
        name="attend",
    )(cache_len, query_lat, jnp.swapaxes(kv_cache, 1, 2), *after)


def hold_kernel(weight, *refs):
    refs[-1][...] = jnp.zeros(refs[-1].shape, refs[-1].dtype)


def hold(weight, *after):
    return pl.pallas_call(
        hold_kernel,
        in_specs=[HELD] + [ANYWHERE] * len(after),
        out_specs=HELD,
        out_shape=jax.ShapeDtypeStruct((8, 128), jnp.float32),
        compiler_params=pltpu.CompilerParams(vmem_limit_bytes=1 * 2**20),
        cost_estimate=pl.CostEstimate(
            flops=0, bytes_accessed=2 * math.prod(weight.shape), transcendentals=0
        ),
        name="hold",
    )(weight, *after)


def expert_kernel(sizes, sizes_out, n_experts, steps, me, w_gate, w_up, w_down, *refs):
    xs = refs[: len(sizes)]
    outs = refs[-4 - len(sizes_out) : -4]
    acc_gate, acc_up, hidden, coef = refs[-4:]
    width = w_gate.shape[1]
    chunk = width // steps
    part = [pl.ds(k * chunk, chunk) for k in range(steps)]
    tail = jnp.concatenate([x[:, width:] for x in xs], axis=0).astype(jnp.float32)
    lane = lax.broadcasted_iota(jnp.int32, tail.shape, 1)
    mine = (lane == me[0]) | (lane == me[0] + n_experts)
    picked = jnp.sum(jnp.where(mine, tail, 0.0), axis=1, keepdims=True)
    coef[...] = jnp.broadcast_to(picked, coef.shape)
    for k in range(steps):
        xk = jnp.concatenate([x[:, part[k]] for x in xs], axis=0)
        g = jnp.dot(xk, w_gate[0, part[k], :], preferred_element_type=jnp.float32)
        u = jnp.dot(xk, w_up[0, part[k], :], preferred_element_type=jnp.float32)
        if k == 0:
            acc_gate[...] = g
            acc_up[...] = u
        else:
            acc_gate[...] += g
            acc_up[...] += u
    g = acc_gate[...]
    hidden[...] = (g / (1.0 + jnp.exp(-g)) * acc_up[...]).astype(jnp.bfloat16)
    for k in range(steps):
        yk = jnp.dot(hidden[...], w_down[0, :, part[k]], preferred_element_type=jnp.float32)
        yk = (yk * coef[:, :1]).astype(jnp.bfloat16)
        row = 0
        for out in outs:
            out[:, part[k]] = yk[row : row + out.shape[0]]
            row += out.shape[0]


def expert_group(xs, slots, gate_weight, up_weight, down_weight, n_experts, *after):
    sizes = [x.shape[0] for x in xs]
    m = sum(sizes)
    _, width, hidden_width = gate_weight.shape
    chunk = max(c for c in range(128, 1025, 128) if width % c == 0)
    steps = width // chunk
    quarter = m // slots // 4
    outs = [quarter] * (2 * slots) + [2 * quarter] * slots
    me = lax.axis_index("dev").astype(jnp.int32).reshape(1)
    return pl.pallas_call(
        functools.partial(expert_kernel, sizes, outs, n_experts, steps),
        in_specs=[SCALARS] + [HELD] * 3 + [HELD] * len(xs) + [ANYWHERE] * len(after),
        out_specs=[HELD] * len(outs),
        scratch_shapes=[
            pltpu.VMEM((m, hidden_width), jnp.float32),
            pltpu.VMEM((m, hidden_width), jnp.float32),
            pltpu.VMEM((m, hidden_width), jnp.bfloat16),
            pltpu.VMEM((m, 128), jnp.float32),
        ],
        out_shape=[jax.ShapeDtypeStruct((r, width), jnp.bfloat16) for r in outs],
        compiler_params=pltpu.CompilerParams(vmem_limit_bytes=8 * 2**20),
        cost_estimate=pl.CostEstimate(
            flops=6 * m * width * hidden_width,
            bytes_accessed=1,
            transcendentals=m * hidden_width,
        ),
        name="experts",
    )(me, gate_weight, up_weight, down_weight, *xs, *after)


def routed_dense(hidden_in, expert_ids, gate_coef, gate_weight, up_weight, down_weight):
    n_dev = lax.axis_size("dev")
    mv = Moves(n_dev)
    weights = (gate_weight, up_weight, down_weight)
    n = mv.line
    half = n // 2
    cat = lambda *a: jnp.concatenate(a, axis=0)
    block = {0: pack_rows(hidden_in, expert_ids, gate_coef, n_dev)}
    arrival = sorted(range(n), key=lambda k: (min(k, n - k), k))
    for k in arrival[1:]:
        block[k] = mv.ring(block[k - 1]) if 2 * k <= n else mv.ring_back(block[(k + 1) % n])
    near = {k: cat(block[k], mv.first(block[k])) for k in arrival}
    far = {k: mv.second(near[k]) for k in arrival}
    own = cat(*[a for k in range(half) for a in (near[k], far[k])])
    held = [hold(w, a) for w, a in zip(weights, (near[0], block[2], near[arrival[2]]))]
    early = expert_group([own, mv.core(own)], half, *weights, n_dev, *held)
    rows = block[0].shape[0]
    order = list(range(1, n)) + [0]
    mine, crossed, back = {}, {}, []
    for k in [k for k in order if k < half]:
        mine[k] = mv.core(early[2 * half + k])
        back.append(plus(early[2 * k + 1], mine[k][2 * rows :]))
        crossed[k] = mv.second(back[-1])
    last = arrival[-1]
    late = [cat(near[k], far[k]) for k in arrival[half:-1]] + [near[last], far[last]]
    theirs = [mv.core(a) for a in late[:-1]] + [mv.core(after(late[-1], early[-1]))]
    late = expert_group(late + theirs, n - half, *weights, n_dev, *back)
    spot = {k: i for i, k in enumerate(arrival[half:])}
    acc = ()
    for k in order:
        if k >= half:
            i = spot[k]
            mine[k] = mv.core(late[2 * (n - half) + i])
            back = plus(late[2 * i + 1], mine[k][2 * rows :])
            crossed[k] = mv.second(after(back, crossed[k - 1]) if k > half else back)
        close = late[2 * spot[k]] if k >= half else early[2 * k]
        side = mv.first(plus(close[rows:], mine[k][rows : 2 * rows], crossed[k][rows:]))
        total = plus(close[:rows], mine[k][:rows], crossed[k][:rows], side, *acc)
        if k:
            acc = (mv.ring(total),)
    return total


def per_device(
    hidden_in,
    expert_ids,
    gate_coef,
    query_lat,
    kv_cache,
    cache_len,
    gate_weight,
    up_weight,
    down_weight,
):
    half_rows = hidden_in.shape[0] // 2
    expert_count = lax.axis_size("dev")
    capacity = max(2, 2 * TOP * half_rows // expert_count)
    weights = (gate_weight, up_weight, down_weight)
    if capacity < half_rows:
        routed_out = routed_sparse(
            hidden_in, expert_ids, gate_coef, *weights, half_rows, capacity
        )
        attention = attend(query_lat, kv_cache, cache_len)
    else:
        routed_out = routed_dense(hidden_in, expert_ids, gate_coef, *weights)
        attention = attend_rows(query_lat, kv_cache, cache_len)
    return (attention, routed_out)


def solution(mesh):
    in_specs = (
        P(("sec", "dev"), None),
        P(("sec", "dev"), None),
        P(("sec", "dev"), None),
        P(("sec", "dev"), None, None),
        P(("sec", "dev"), None, None),
        P(("sec", "dev")),
        P("dev", None, "sec"),
        P("dev", None, "sec"),
        P("dev", "sec", None),
    )
    out_specs = (P(("sec", "dev"), None, None), P(("sec", "dev"), None))
    return jax.shard_map(
        per_device, mesh=mesh, in_specs=in_specs, out_specs=out_specs, check_vma=False
    )
```

```python
import functools
import math

import jax
import jax.numpy as jnp
from jax import lax
from jax.experimental import pallas as pl
from jax.experimental.pallas import tpu as pltpu
from jax.sharding import PartitionSpec as P

LAT = 512
TOP = 8
AXES = ("sec", "dev")

score_scale = 1.0 / math.sqrt(192.0)


def attend(query_lat, kv_cache, cache_len):
    scores = (
        jnp.einsum("rhk,rlk->rhl", query_lat, kv_cache, preferred_element_type=jnp.float32)
        * score_scale
    )
    positions = jnp.arange(kv_cache.shape[1], dtype=jnp.int32)
    visible = positions[None, None, :] < cache_len[:, None, None]
    scores = jnp.where(visible, scores, jnp.float32(-1e30))
    top_score = jnp.max(scores, axis=2, keepdims=True)
    exponent = jnp.exp(scores - top_score)
    denominator = jnp.sum(exponent, axis=2, keepdims=True)
    weights = (exponent / denominator).astype(jnp.bfloat16)
    return jnp.einsum(
        "rhl,rlc->rhc", weights, kv_cache[:, :, :LAT], preferred_element_type=jnp.float32
    ).astype(jnp.bfloat16)


def routing_tables(expert_ids, gate_coef, expert_count, capacity):
    row_count, top_count = expert_ids.shape
    flat_ids = expert_ids.reshape(-1)
    position_ids = jnp.arange(flat_ids.shape[0], dtype=jnp.int32)
    matches = (flat_ids[:, None] == flat_ids[None, :]) & (
        position_ids[None, :] < position_ids[:, None]
    )
    slot_rank = jnp.sum(matches.astype(jnp.int32), axis=1)
    target = flat_ids * capacity + slot_rank
    slot_ids = jnp.arange(expert_count * capacity, dtype=jnp.int32)
    placed = (target[None, :] == slot_ids[:, None]).astype(jnp.float32)
    owner_hot = (
        (position_ids // top_count)[:, None] == jnp.arange(row_count, dtype=jnp.int32)[None, :]
    ).astype(jnp.float32)
    picker = jnp.dot(placed, owner_hot, precision=lax.Precision.HIGHEST).astype(jnp.bfloat16)
    weighted = owner_hot * gate_coef.reshape(-1)[:, None]
    mixing = jnp.dot(weighted.T, placed.T, precision=lax.Precision.HIGHEST)
    return (picker, mixing)


def expert_rows(tokens, gate_weight, up_weight, down_weight):
    shape_in = tokens.shape
    flat_rows = tokens.reshape(-1, shape_in[-1])
    gate_val = jnp.dot(flat_rows, gate_weight[0], preferred_element_type=jnp.float32)
    up_val = jnp.dot(flat_rows, up_weight[0], preferred_element_type=jnp.float32)
    hidden = (jax.nn.silu(gate_val) * up_val).astype(jnp.bfloat16)
    part_out = jnp.dot(hidden, down_weight[0], preferred_element_type=jnp.float32).astype(
        jnp.bfloat16
    )
    return part_out.reshape(shape_in)


def route_tokens(send_buf, gate_weight, up_weight, down_weight):
    section_count = lax.axis_size("sec")
    doubled = jnp.concatenate([send_buf] * section_count, axis=0)
    halves = expert_rows(
        lax.all_to_all(doubled, AXES, split_axis=0, concat_axis=0, tiled=True),
        gate_weight,
        up_weight,
        down_weight,
    )
    returned = lax.all_to_all(halves, AXES, split_axis=0, concat_axis=0, tiled=True)
    pieces = returned.reshape((section_count,) + send_buf.shape).astype(jnp.float32)
    return jnp.sum(pieces, axis=0).astype(jnp.bfloat16)


def combine(returned, mixing):
    flat_back = returned.reshape(-1, returned.shape[-1]).astype(jnp.float32)
    return jnp.dot(mixing, flat_back, precision=lax.Precision.HIGHEST).astype(jnp.bfloat16)


def routed_sparse(
    hidden_in, expert_ids, gate_coef, gate_weight, up_weight, down_weight, half_rows, capacity
):
    model_width = hidden_in.shape[1]
    expert_count = lax.axis_size("dev")
    outs = []
    for offset in (0, half_rows):
        picker, mixing = routing_tables(
            expert_ids[offset : offset + half_rows],
            gate_coef[offset : offset + half_rows],
            expert_count,
            capacity,
        )
        gathered = jnp.dot(
            picker, hidden_in[offset : offset + half_rows], preferred_element_type=jnp.float32
        ).astype(jnp.bfloat16)
        send_buf = gathered.reshape(expert_count, capacity, model_width)
        outs.append(combine(route_tokens(send_buf, gate_weight, up_weight, down_weight), mixing))
    return jnp.concatenate(outs, axis=0)


def permutation(n_dev, move):
    pairs = []
    for y in range(2):
        for d in range(n_dev):
            there = move(y, d // 4, (d // 2) % 2, d % 2)
            if there is not None:
                ty, tz, tx, tc = there
                pairs.append((y * n_dev + d, ty * n_dev + tz * 4 + tx * 2 + tc))
    return lambda a: lax.ppermute(a, AXES, pairs)


class Moves:
    def __init__(self, n_dev):
        line = n_dev // 4
        self.line = line
        self.core = permutation(n_dev, lambda y, z, x, c: (y, z, x, 1 - c))
        self.first = permutation(
            n_dev, lambda y, z, x, c: (1 - y, z, x, c) if c else (y, z, 1 - x, c)
        )
        self.second = permutation(
            n_dev, lambda y, z, x, c: (y, z, 1 - x, c) if c else (1 - y, z, x, c)
        )
        stops = list(range(0, line, 2)) + list(range(1, line, 2))[::-1]
        following = {z: stops[(i + 1) % line] for i, z in enumerate(stops)}
        before = {t: z for z, t in following.items()}
        self.ring = permutation(n_dev, lambda y, z, x, c: (y, following[z], x, c))
        self.ring_back = permutation(n_dev, lambda y, z, x, c: (y, before[z], x, c))


def plus(*terms):
    total = terms[0].astype(jnp.float32)
    for t in terms[1:]:
        total = total + t.astype(jnp.float32)
    return total.astype(jnp.bfloat16)


def after(a, other):
    return a + other[:1, :1] * 0


ANYWHERE = pl.BlockSpec(memory_space=pl.ANY)
FAR = pl.BlockSpec(memory_space=pltpu.HBM)
HELD = pl.BlockSpec(memory_space=pltpu.VMEM)
SCALARS = pl.BlockSpec(memory_space=pltpu.SMEM)


def pack_kernel(n_experts, ids, coefs, x, out):
    rows, width = x.shape
    hot = lax.broadcasted_iota(jnp.int32, (n_experts, rows), 0)
    dense = jnp.zeros((n_experts, rows), jnp.float32)
    for k in range(ids.shape[0]):
        dense += jnp.where(hot == ids[k : k + 1, :], coefs[k : k + 1, :], 0.0)
    high = dense.astype(jnp.bfloat16)
    low = (dense - high.astype(jnp.float32)).astype(jnp.bfloat16)
    rest = jnp.zeros((out.shape[1] - width - 2 * n_experts, rows), jnp.bfloat16)
    parts = jnp.concatenate([high, low, rest], axis=0)
    same = lax.broadcasted_iota(jnp.int32, (rows, rows), 0) == lax.broadcasted_iota(
        jnp.int32, (rows, rows), 1
    )
    turned = lax.dot_general(
        same.astype(jnp.bfloat16),
        parts,
        (((1,), (1,)), ((), ())),
        preferred_element_type=jnp.float32,
    )
    out[:, :width] = x[...]
    out[:, width:] = turned.astype(jnp.bfloat16)


def pack_rows(hidden_in, expert_ids, gate_coef, n_experts):
    rows, width = hidden_in.shape
    tail = 2 * n_experts + -2 * n_experts % 128
    return pl.pallas_call(
        functools.partial(pack_kernel, n_experts),
        in_specs=[HELD] * 3,
        out_specs=HELD,
        out_shape=jax.ShapeDtypeStruct((rows, width + tail), jnp.bfloat16),
        name="pack",
    )(expert_ids.T, gate_coef.T, hidden_in)


def attend_kernel(lengths, q, kv, *refs):
    out = refs[-1]
    rows, heads, _ = q.shape
    slots = kv.shape[2]
    base = pl.program_id(0) * rows
    position = lax.broadcasted_iota(jnp.int32, (heads, slots), 1)
    scores = []
    for r in range(rows):
        s = jnp.dot(q[r], kv[r], preferred_element_type=jnp.float32) * score_scale
        scores.append(jnp.where(position < lengths[base + r], s, -1e30))
    scores = jnp.concatenate(scores, axis=0)
    exponent = jnp.exp(scores - jnp.max(scores, axis=1, keepdims=True))
    weights = exponent / jnp.sum(exponent, axis=1, keepdims=True)
    weights = weights.astype(jnp.bfloat16)
    for r in range(rows):
        out[r] = lax.dot_general(
            weights[r * heads : (r + 1) * heads],
            kv[r, : out.shape[2]],
            (((1,), (1,)), ((), ())),
            preferred_element_type=jnp.float32,
        ).astype(jnp.bfloat16)


def attend_rows(query_lat, kv_cache, cache_len, *after):
    rows, heads, width = query_lat.shape
    slots = kv_cache.shape[1]
    step = max(s for s in (8, 1) if rows % s == 0)
    return pl.pallas_call(
        attend_kernel,
        grid=(rows // step,),
        in_specs=[
            SCALARS,
            pl.BlockSpec((step, heads, width), lambda i: (i, 0, 0)),
            pl.BlockSpec((step, width, slots), lambda i: (i, 0, 0)),
        ]
        + [ANYWHERE] * len(after),
        out_specs=pl.BlockSpec((step, heads, LAT), lambda i: (i, 0, 0)),
        out_shape=jax.ShapeDtypeStruct((rows, heads, LAT), jnp.bfloat16),
        compiler_params=pltpu.CompilerParams(vmem_limit_bytes=40 * 2**20),
        cost_estimate=pl.CostEstimate(
            flops=20 * rows * heads * slots * (width + LAT), bytes_accessed=1, transcendentals=0
        ),
        name="attend",
    )(cache_len, query_lat, jnp.swapaxes(kv_cache, 1, 2), *after)


def hold_kernel(weight, *refs):
    refs[-1][...] = jnp.zeros(refs[-1].shape, refs[-1].dtype)


def hold(weight, *after):
    return pl.pallas_call(
        hold_kernel,
        in_specs=[HELD] + [ANYWHERE] * len(after),
        out_specs=HELD,
        out_shape=jax.ShapeDtypeStruct((8, 128), jnp.float32),
        compiler_params=pltpu.CompilerParams(vmem_limit_bytes=1 * 2**20),
        cost_estimate=pl.CostEstimate(
            flops=0, bytes_accessed=2 * math.prod(weight.shape), transcendentals=0
        ),
        name="hold",
    )(weight, *after)


def expert_kernel(sizes, sizes_out, n_experts, steps, me, w_gate, w_up, w_down, *refs):
    xs = refs[: len(sizes)]
    outs = refs[-4 - len(sizes_out) : -4]
    acc_gate, acc_up, hidden, coef = refs[-4:]
    width = w_gate.shape[1]
    chunk = width // steps
    part = [pl.ds(k * chunk, chunk) for k in range(steps)]
    tail = jnp.concatenate([x[:, width:] for x in xs], axis=0).astype(jnp.float32)
    lane = lax.broadcasted_iota(jnp.int32, tail.shape, 1)
    mine = (lane == me[0]) | (lane == me[0] + n_experts)
    picked = jnp.sum(jnp.where(mine, tail, 0.0), axis=1, keepdims=True)
    coef[...] = jnp.broadcast_to(picked, coef.shape)
    for k in range(steps):
        xk = jnp.concatenate([x[:, part[k]] for x in xs], axis=0)
        g = jnp.dot(xk, w_gate[0, part[k], :], preferred_element_type=jnp.float32)
        u = jnp.dot(xk, w_up[0, part[k], :], preferred_element_type=jnp.float32)
        if k == 0:
            acc_gate[...] = g
            acc_up[...] = u
        else:
            acc_gate[...] += g
            acc_up[...] += u
    g = acc_gate[...]
    hidden[...] = (g / (1.0 + jnp.exp(-g)) * acc_up[...]).astype(jnp.bfloat16)
    for k in range(steps):
        yk = jnp.dot(hidden[...], w_down[0, :, part[k]], preferred_element_type=jnp.float32)
        yk = (yk * coef[:, :1]).astype(jnp.bfloat16)
        row = 0
        for out in outs:
            out[:, part[k]] = yk[row : row + out.shape[0]]
            row += out.shape[0]


def expert_group(xs, slots, gate_weight, up_weight, down_weight, n_experts, *after):
    sizes = [x.shape[0] for x in xs]
    m = sum(sizes)
    _, width, hidden_width = gate_weight.shape
    chunk = max(c for c in range(128, 1025, 128) if width % c == 0)
    steps = width // chunk
    quarter = m // slots // 4
    outs = [quarter] * (2 * slots) + [2 * quarter] * slots
    me = lax.axis_index("dev").astype(jnp.int32).reshape(1)
    return pl.pallas_call(
        functools.partial(expert_kernel, sizes, outs, n_experts, steps),
        in_specs=[SCALARS] + [HELD] * 3 + [HELD] * len(xs) + [ANYWHERE] * len(after),
        out_specs=[HELD] * len(outs),
        scratch_shapes=[
            pltpu.VMEM((m, hidden_width), jnp.float32),
            pltpu.VMEM((m, hidden_width), jnp.float32),
            pltpu.VMEM((m, hidden_width), jnp.bfloat16),
            pltpu.VMEM((m, 128), jnp.float32),
        ],
        out_shape=[jax.ShapeDtypeStruct((r, width), jnp.bfloat16) for r in outs],
        compiler_params=pltpu.CompilerParams(vmem_limit_bytes=8 * 2**20),
        cost_estimate=pl.CostEstimate(
            flops=6 * m * width * hidden_width,
            bytes_accessed=1,
            transcendentals=m * hidden_width,
        ),
        name="experts",
    )(me, gate_weight, up_weight, down_weight, *xs, *after)


def routed_dense(hidden_in, expert_ids, gate_coef, gate_weight, up_weight, down_weight):
    n_dev = lax.axis_size("dev")
    mv = Moves(n_dev)
    weights = (gate_weight, up_weight, down_weight)
    n = mv.line
    half = n // 2
    cat = lambda *a: jnp.concatenate(a, axis=0)
    block = {0: pack_rows(hidden_in, expert_ids, gate_coef, n_dev)}
    arrival = sorted(range(n), key=lambda k: (min(k, n - k), k))
    for k in arrival[1:]:
        block[k] = mv.ring(block[k - 1]) if 2 * k <= n else mv.ring_back(block[(k + 1) % n])
    near = {k: cat(block[k], mv.first(block[k])) for k in arrival}
    far = {k: mv.second(near[k]) for k in arrival}
    own = cat(*[a for k in range(half) for a in (near[k], far[k])])
    held = [hold(w, a) for w, a in zip(weights, (near[0], block[2], near[arrival[2]]))]
    early = expert_group([own, mv.core(own)], half, *weights, n_dev, *held)
    rows = block[0].shape[0]
    order = list(range(1, n)) + [0]
    mine, crossed, back = {}, {}, []
    for k in [k for k in order if k < half]:
        mine[k] = mv.core(early[2 * half + k])
        back.append(plus(early[2 * k + 1], mine[k][2 * rows :]))
        crossed[k] = mv.second(back[-1])
    last = arrival[-1]
    late = [cat(near[k], far[k]) for k in arrival[half:-1]] + [near[last], far[last]]
    theirs = [mv.core(a) for a in late[:-1]] + [mv.core(after(late[-1], early[-1]))]
    late = expert_group(late + theirs, n - half, *weights, n_dev, *back)
    spot = {k: i for i, k in enumerate(arrival[half:])}
    acc = ()
    for k in order:
        if k >= half:
            i = spot[k]
            mine[k] = mv.core(late[2 * (n - half) + i])
            back = plus(late[2 * i + 1], mine[k][2 * rows :])
            crossed[k] = mv.second(back + crossed[k - 1] * 0 if k > half else back)
        close = late[2 * spot[k]] if k >= half else early[2 * k]
        side = mv.first(plus(close[rows:], mine[k][rows : 2 * rows], crossed[k][rows:]))
        total = plus(close[:rows], mine[k][:rows], crossed[k][:rows], side, *acc)
        if k:
            acc = (mv.ring(total),)
    return total


def per_device(
    hidden_in,
    expert_ids,
    gate_coef,
    query_lat,
    kv_cache,
    cache_len,
    gate_weight,
    up_weight,
    down_weight,
):
    half_rows = hidden_in.shape[0] // 2
    expert_count = lax.axis_size("dev")
    capacity = max(2, 2 * TOP * half_rows // expert_count)
    weights = (gate_weight, up_weight, down_weight)
    if capacity < half_rows:
        routed_out = routed_sparse(
            hidden_in, expert_ids, gate_coef, *weights, half_rows, capacity
        )
        attention = attend(query_lat, kv_cache, cache_len)
    else:
        routed_out = routed_dense(hidden_in, expert_ids, gate_coef, *weights)
        attention = attend_rows(query_lat, kv_cache, cache_len)
    return (attention, routed_out)


def solution(mesh):
    in_specs = (
        P(("sec", "dev"), None),
        P(("sec", "dev"), None),
        P(("sec", "dev"), None),
        P(("sec", "dev"), None, None),
        P(("sec", "dev"), None, None),
        P(("sec", "dev")),
        P("dev", None, "sec"),
        P("dev", None, "sec"),
        P("dev", "sec", None),
    )
    out_specs = (P(("sec", "dev"), None, None), P(("sec", "dev"), None))
    return jax.shard_map(
        per_device, mesh=mesh, in_specs=in_specs, out_specs=out_specs, check_vma=False
    )
```
